32 devices in a mesh: ta: 4 (over y, x), ha: 2 (over core), wa: 4 (over z).
Axes of the slice: x: 2, y: 2, z: 4, core: 2. Of those that a mesh axis runs over, the one named last changes fastest.
Arguments:
- latents: bfloat16 [8, 32, 128, 256], P('ta', 'ha', 'wa'), may hold values from -6 to 6
- norm_gain: float32 [256], replicated, may hold values from 0.1 to 1.9
- conv_weight: bfloat16 [3, 3, 3, 256, 256], replicated, may hold values from -0.078125 to 0.078125
- qkv_weight: bfloat16 [1024, 16, 3, 128], P(None, ('ta', 'wa')), may hold values from -2.7 to 2.7
Outputs:
- block_out: bfloat16 [8, 32, 128, 256], P('ta', 'ha', 'wa')
- attended: bfloat16 [8, 16, 64, 16, 128], P(None, 'ha', None, ('ta', 'wa'))
The draws below stay inside these ranges and needn't reach their ends.
All inputs are finite; a program needn't handle non-finite values.
Results may differ from the reference program's by a relative error of at most 0.0062.
Values may be sent and summed in bfloat16 or wider, within the bound.
A program may use at most 128 MiB of HBM per device.

```python
import jax
import jax.numpy as jnp
from jax import lax

C = 256
HD = 128
WIN = 4
HEADS = 16
PD = 1024
NT = 8
NH = 32
NW = 128
PR = 16
PC = 64


def draw_qkv_weight(key, part):
    base = jax.random.truncated_normal(key, -6.0, 6.0, (PD, HEADS, 3, HD), jnp.float32) / PD ** 0.5
    return base.astype(jnp.bfloat16)


def block_scale(stream_key, shape, pieces, smallest, high):
    def one(dim, shards_of):
        steps = jax.random.uniform(jax.random.fold_in(jax.random.fold_in(stream_key, 6), dim), (shards_of,), jnp.float32, smallest / len(pieces), high / len(pieces))
        return jnp.repeat(jnp.exp(steps), shape[dim] // shards_of).reshape((-1,) + (1,) * (len(shape) - dim - 1))

    factor_of = one(*pieces[0])
    for cut in pieces[1:]:
        factor_of = factor_of * one(*cut)
    return factor_of


def gaussian(own_key, shape, width, limit, shards=(), held_as=jnp.bfloat16):
    entries = width * jax.random.normal(own_key, shape, jnp.float32)
    if shards:
        entries = entries * block_scale(own_key, shape, shards, -0.22, 0.18)
    return jnp.clip(entries, -limit, limit).astype(held_as)


def setup_inputs(seed: int = 0) -> dict:
    arg_keys = jax.random.split(jax.random.key(seed), 5)
    latents = gaussian(arg_keys[0], (NT, NH, NW, C), 1.0, 6.0, ((0, 4), (1, 2), (2, 4)))
    norm_gain = jnp.clip(1.0 + 0.18 * jax.random.normal(arg_keys[1], (C,), jnp.float32), 0.1, 1.9)
    conv_weight = gaussian(arg_keys[2], (3, 3, 3, C, C), (27 * C) ** -0.5, 0.078125)
    qkv_weight = draw_qkv_weight(jax.random.fold_in(arg_keys[4], 71), 0)
    return dict(latents=latents, norm_gain=norm_gain, conv_weight=conv_weight, qkv_weight=qkv_weight)


def reference(latents, norm_gain, conv_weight, qkv_weight):
    latent_f32 = latents.astype(jnp.float32)
    scale_rms = lax.rsqrt(lax.optimization_barrier(jnp.mean(latent_f32 * latent_f32, axis=-1, keepdims=True)) + 1e-06)
    normed = jax.nn.silu(latent_f32 * scale_rms * norm_gain).astype(jnp.bfloat16)
    conv_out = lax.conv_general_dilated(normed.astype(jnp.float32)[None], conv_weight.astype(jnp.float32), (1, 1, 1), 'SAME', dimension_numbers=('NDHWC', 'DHWIO', 'NDHWC'), precision=lax.Precision.HIGHEST)[0]
    block_out = (latent_f32 + conv_out).astype(jnp.bfloat16)
    patches = block_out.reshape(NT, PR, 2, PC, 2, C).transpose(0, 1, 3, 2, 4, 5).reshape(NT * PR * PC, PD).astype(jnp.float32)
    band_count = PR // WIN
    offsets = jnp.arange(3 * WIN, dtype=jnp.int32) - WIN
    q_row = jnp.arange(WIN, dtype=jnp.int32)[:, None]
    band_rows = jnp.arange(band_count, dtype=jnp.int32)[:, None, None] * WIN + offsets[None, None, :]
    allowed = (jnp.abs(q_row - offsets[None, :]) <= WIN)[None] & (band_rows >= 0) & (band_rows < PR)
    gather_rows = (jnp.arange(band_count, dtype=jnp.int32)[:, None] * WIN + jnp.arange(3 * WIN, dtype=jnp.int32)[None, :]).astype(jnp.int32)

    def one_head(head_weight):
        qkv_rows = jnp.dot(patches, head_weight.reshape(PD, 3 * HD).astype(jnp.float32), precision=lax.Precision.HIGHEST).astype(jnp.bfloat16)
        qkv_rows = lax.optimization_barrier(qkv_rows).astype(jnp.float32).reshape(NT, PR, PC, 3, HD)
        queries = qkv_rows[:, :, :, 0].reshape(NT, band_count, WIN, PC, HD)
        padded = jnp.pad(qkv_rows[:, :, :, 1:], ((0, 0), (WIN, WIN), (0, 0), (0, 0), (0, 0)))
        banded = jnp.take(padded, gather_rows, axis=1)
        scores = jnp.einsum('tniad,tnjbd->tniajb', queries, banded[..., 0, :], precision=lax.Precision.HIGHEST) * HD ** (-0.5)
        scores = jnp.where(allowed[None, :, :, None, :, None], scores, -1e+30)
        row_max = lax.optimization_barrier(jnp.max(scores, axis=(4, 5), keepdims=True))
        exp_scores = jnp.exp(scores - row_max)
        probs = (exp_scores / lax.optimization_barrier(jnp.sum(exp_scores, axis=(4, 5), keepdims=True))).astype(jnp.bfloat16)
        probs = lax.optimization_barrier(probs).astype(jnp.float32)
        result = jnp.einsum('tniajb,tnjbd->tniad', probs, banded[..., 1, :], precision=lax.Precision.HIGHEST)
        return result.astype(jnp.bfloat16).reshape(NT, PR, PC, HD)
    heads_out = lax.map(one_head, qkv_weight.transpose(1, 0, 2, 3))
    attended = heads_out.transpose(1, 2, 3, 0, 4)
    return (block_out, attended)
```

```python
import functools

import jax
import jax.numpy as jnp
from jax import lax
from jax.experimental import pallas as pl
from jax.experimental.pallas import tpu as pltpu
from jax.sharding import PartitionSpec as P

WIN = 4
CH = 8
MESH = pl.DeviceIdType.MESH
F32 = jnp.float32
BF16 = jnp.bfloat16


def kernel(n_t, n_h, n_w, normed, cols, latents, cw_hbm, w_hbm, out_block, out_att,
           pad_n, pad_c, cf, x3, cw, wg, fbuf, pat, q_buf, kv, bias, o_buf,
           loc_sem, halo_s, halo_r, w_s, w_r, ag_s, ag_r, kv_s, kv_r, at_s, at_r):
    t_dev, h_dev, w_dev, ch = latents.shape
    rows = h_dev // 2
    cols_dev = w_dev // 2
    hd = q_buf.shape[-1]
    pc = n_w * cols_dev
    cpt = h_dev // CH
    prow = CH // 2
    it, ih, iw = lax.axis_index("ta"), lax.axis_index("ha"), lax.axis_index("wa")
    has = {"t-": it > 0, "t+": it < n_t - 1, "h-": ih > 0, "h+": ih < n_h - 1,
           "w-": iw > 0, "w+": iw < n_w - 1}
    opp = {"-": "+", "+": "-"}
    dev = {"t-": {"ta": it - 1}, "t+": {"ta": it + 1}, "h-": {"ha": ih - 1}, "h+": {"ha": ih + 1},
           "w-": {"wa": iw - 1}, "w+": {"wa": iw + 1}}

    def rcopy(src, dst, ss, rs, device):
        return pltpu.make_async_remote_copy(
            src_ref=src, dst_ref=dst, send_sem=ss, recv_sem=rs, device_id=device, device_id_type=MESH)

    cw_copy = pltpu.make_async_copy(cw_hbm, cw, loc_sem.at[0])
    cw_copy.start()
    own_w = pltpu.make_async_copy(w_hbm, wg.at[it], loc_sem.at[1])
    own_w.start()

    bar = pltpu.get_barrier_semaphore()
    count = jnp.int32(n_t - 1)
    for side in ("h-", "h+", "w-", "w+"):
        count = count + has[side].astype(jnp.int32)

        @pl.when(has[side])
        def _():
            pl.semaphore_signal(bar, inc=1, device_id=dev[side], device_id_type=MESH)
    for d in range(1, n_t):
        pl.semaphore_signal(bar, inc=1, device_id={"ta": lax.rem(it + d, n_t)}, device_id_type=MESH)
    pl.semaphore_wait(bar, count)

    def halo(i, side, src, dst):
        c = rcopy(src, dst, halo_s.at[i], halo_r.at[i], dev[side])
        from_side = side[0] + opp[side[1]]

        def start():
            @pl.when(has[side])
            def _():
                c.start()

        def recv():
            @pl.when(has[from_side])
            def _():
                c.wait_recv()

        def sent():
            @pl.when(has[side])
            def _():
                c.wait_send()
        return start, recv, sent

    own = pl.ds(h_dev, h_dev)
    ph_w = [halo(0, "w-", cols.at[0], pad_c.at[1, pl.ds(1, t_dev), own]),
            halo(1, "w+", cols.at[1], pad_c.at[0, pl.ds(1, t_dev), own])]
    ph_t = [halo(2, "t-", normed.at[0], pad_n.at[t_dev + 1, pl.ds(1, h_dev)]),
            halo(3, "t+", normed.at[t_dev - 1], pad_n.at[0, pl.ds(1, h_dev)])]
    ph_wt = [halo(4, "t-", pad_c.at[:, 1, own], pad_c.at[:, t_dev + 1, own]),
             halo(5, "t+", pad_c.at[:, t_dev, own], pad_c.at[:, 0, own])]
    ph_h = [halo(6, "h-", pad_n.at[:, 1], pad_n.at[:, h_dev + 1]),
            halo(7, "h+", pad_n.at[:, h_dev], pad_n.at[:, 0]),
            halo(8, "h-", pad_c.at[:, :, own], pad_c.at[:, :, pl.ds(2 * h_dev, h_dev)]),
            halo(9, "h+", pad_c.at[:, :, own], pad_c.at[:, :, pl.ds(0, h_dev)])]
    for s in ph_w + ph_t:
        s[0]()

    for d in range(1, n_t):
        rcopy(w_hbm, wg.at[it], w_s.at[d], w_r.at[d], {"ta": lax.rem(it + d, n_t)}).start()

    def zero(cond, ref, idx, shape):
        @pl.when(cond)
        def _():
            ref[idx] = jnp.zeros(shape, ref.dtype)

    no = {k: jnp.logical_not(v) for k, v in has.items()}
    full = slice(None)
    for side, s in (("w-", 0), ("w+", 1)):
        zero(no[side], pad_c, (s, pl.ds(1, t_dev), own), (t_dev, h_dev, ch))
    for side, t in (("t-", 0), ("t+", t_dev + 1)):
        zero(no[side], pad_c, (full, t, own), (2, h_dev, ch))
        zero(no[side], pad_n, (t, pl.ds(1, h_dev)), (h_dev, w_dev, ch))
    for side, r, b in (("h-", 0, 0), ("h+", h_dev + 1, 2 * h_dev)):
        zero(no[side], pad_n, (full, r), (t_dev + 2, w_dev, ch))
        zero(no[side], pad_c, (full, full, pl.ds(b, h_dev)), (2, t_dev + 2, h_dev, ch))
        zero(no[side], kv, (full, pl.ds(0 if side == "h-" else rows + WIN, WIN)),
             (t_dev, WIN) + kv.shape[2:])
    pad_n[pl.ds(1, t_dev), pl.ds(1, h_dev)] = normed[...]

    total_rows = rows * n_h
    bs = (WIN * pc, 3 * WIN * pc)
    qr = lax.broadcasted_iota(jnp.int32, bs, 0) // pc
    kr = lax.broadcasted_iota(jnp.int32, bs, 1) // pc - WIN
    for b in range(rows // WIN):
        kg = ih * rows + b * WIN + kr
        ok = (jnp.abs(qr - kr) <= WIN) & (kg >= 0) & (kg < total_rows)
        bias[b] = jnp.where(ok, 0.0, -1e30).astype(F32)

    for s in ph_w:
        s[1]()
    for s in ph_wt:
        s[0]()
    for s in ph_t + ph_wt:
        s[1]()
    for s in ph_h:
        s[0]()
    for s in ph_h:
        s[1]()

    cf[...] = pad_c[...].astype(F32)
    edge = lax.broadcasted_iota(jnp.int32, (w_dev, ch), 0)

    @pl.loop(0, t_dev + 2)
    def _(t):
        for r in range(h_dev + 2):
            v16 = pad_n[t, r]
            v = v16.astype(F32)
            hr = pl.ds(h_dev - 1 + r, 1)
            left = jnp.where(edge == 0, cf[0, t, hr, :], pltpu.roll(v, 1, 0))
            right = jnp.where(edge == w_dev - 1, cf[1, t, hr, :], pltpu.roll(v, w_dev - 1, 0))
            x3[t, r, :, 0:ch] = left.astype(BF16)
            x3[t, r, :, ch:2 * ch] = v16
            x3[t, r, :, 2 * ch:3 * ch] = right.astype(BF16)

    cw_copy.wait()

    def piece(src, t, i0):
        return pat.at[src, t, pl.ds(i0, prow)]

    sides = (("w+", 0), ("w-", 1))

    @pl.loop(0, t_dev * cpt)
    def _(c):
        t = c // cpt
        h0 = (c % cpt) * CH
        acc = latents[t, pl.ds(h0, CH)].astype(F32).reshape(CH * w_dev, ch)
        for a in range(3):
            for b in range(3):
                acc = acc + jnp.dot(
                    x3[t + a, pl.ds(h0 + b, CH)].reshape(CH * w_dev, 3 * ch), cw[a, b],
                    preferred_element_type=F32)
        blk = acc.astype(BF16)
        out_block[t, pl.ds(h0, CH)] = blk.reshape(CH, w_dev, ch)
        blk = blk.astype(F32)
        for k in range(ch // 128):
            fbuf[k] = blk[:, k * 128:(k + 1) * 128]
        for k in range(ch // 128):
            for dw in range(2):
                part = fbuf[k, pl.ds(dw, CH * cols_dev, stride=2), :].astype(BF16)
                part = part.reshape(prow, 2, cols_dev, 128)
                for dh in range(2):
                    lo = (dh * 2 + dw) * ch + k * 128
                    pat[iw, t, pl.ds((c % cpt) * prow, prow), :, lo:lo + 128] = part[:, dh]
        p = piece(iw, t, (c % cpt) * prow)
        for side, i in sides:
            @pl.when(has[side])
            def _():
                rcopy(p, p, ag_s.at[i, 0, c], ag_r.at[i, 0, c], dev[side]).start()

    def relay(t, d):
        for j in range(cpt):
            c = t * cpt + j
            for side, i in sides:
                src = iw - d if i == 0 else iw + d
                here = src >= 0 if i == 0 else src < n_w
                p = piece(src, t, j * prow)

                @pl.when(here)
                def _():
                    rcopy(p, p, ag_s.at[i, d - 1, c], ag_r.at[i, d - 1, c], dev[side]).wait_recv()
                    if d < n_w - 1:
                        @pl.when(has[side])
                        def _():
                            rcopy(p, p, ag_s.at[i, d, c], ag_r.at[i, d, c], dev[side]).start()

    def qkv(t):
        @pl.loop(0, n_t)
        def _(a):
            x = pat[:, t].reshape(n_w * rows * cols_dev, 4 * ch)
            y = jnp.dot(x, wg[a], preferred_element_type=F32).astype(BF16)
            y = y.reshape(n_w, rows, cols_dev, 3 * hd)
            for s in range(n_w):
                cc = pl.ds(s * cols_dev, cols_dev)
                q_buf[t, a, :, cc, :] = y[s, :, :, 0:hd]
                kv[t, pl.ds(WIN, rows), 2 * a, cc, :] = y[s, :, :, hd:2 * hd]
                kv[t, pl.ds(WIN, rows), 2 * a + 1, cc, :] = y[s, :, :, 2 * hd:3 * hd]

    def rim(t):
        return [("h-", rcopy(kv.at[t, pl.ds(WIN, WIN)], kv.at[t, pl.ds(rows + WIN, WIN)],
                             kv_s.at[t, 0], kv_r.at[t, 0], dev["h-"])),
                ("h+", rcopy(kv.at[t, pl.ds(rows, WIN)], kv.at[t, pl.ds(0, WIN)],
                             kv_s.at[t, 1], kv_r.at[t, 1], dev["h+"]))]

    scale = hd ** (-0.5) * 1.4426950408889634

    def attend(t):
        @pl.loop(0, n_t)
        def _(a):
            for b in range(rows // WIN):
                r = pl.ds(b * WIN, WIN)
                kr_ = pl.ds(b * WIN, 3 * WIN)
                q = q_buf[t, a, r].reshape(WIN * pc, hd)
                k = kv[t, kr_, 2 * a].reshape(3 * WIN * pc, hd)
                v = kv[t, kr_, 2 * a + 1].reshape(3 * WIN * pc, hd)
                s = lax.dot_general(q, k, (((1,), (1,)), ((), ())), preferred_element_type=F32)
                s = s + bias[b]
                m = jnp.max(s, axis=1, keepdims=True)
                e = jnp.exp2((s - m) * scale)
                z = jnp.sum(e, axis=1, keepdims=True)
                o = jnp.dot(e.astype(BF16), v, preferred_element_type=F32) / z
                o_buf[t, a, r] = o.astype(BF16).reshape(WIN, pc, hd)
            dst = out_att.at[it * t_dev + t]

            @pl.when(a != it)
            def _():
                rcopy(o_buf.at[t, a], dst, at_s.at[t, a], at_r.at[t, it], {"ta": a}).start()

            @pl.when(a == it)
            def _():
                pltpu.make_async_copy(o_buf.at[t, a], dst, loc_sem.at[2 + t]).start()

    def weights_in():
        own_w.wait()
        for d in range(1, n_t):
            src = lax.rem(it + n_t - d, n_t)
            rcopy(w_hbm, wg.at[src], w_s.at[d], w_r.at[d], {"ta": src}).wait_recv()

    for d in range(1, n_w):
        relay(0, d)
    weights_in()
    for t in range(t_dev):
        qkv(t)
        for side, c in rim(t):
            @pl.when(has[side])
            def _():
                c.start()
        if t + 1 < t_dev:
            for d in range(1, n_w):
                relay(t + 1, d)
        for side, c in rim(t):
            @pl.when(has[side[0] + opp[side[1]]])
            def _():
                c.wait_recv()
        attend(t)

    for t in range(t_dev):
        pltpu.make_async_copy(o_buf.at[t, it], out_att.at[it * t_dev + t], loc_sem.at[2 + t]).wait()
        for d in range(1, n_t):
            src = lax.rem(it + d, n_t)
            rcopy(o_buf.at[t, src], out_att.at[src * t_dev + t], at_s.at[t, src], at_r.at[t, src],
                  {"ta": src}).wait()
        for side, c in rim(t):
            @pl.when(has[side])
            def _():
                c.wait_send()
    for s in ph_w + ph_t + ph_wt + ph_h:
        s[2]()
    for d in range(1, n_t):
        rcopy(w_hbm, wg.at[it], w_s.at[d], w_r.at[d], {"ta": lax.rem(it + d, n_t)}).wait_send()
    for t in range(t_dev):
        for j in range(cpt):
            c = t * cpt + j
            for side, i in sides:
                for d in range(n_w - 1):
                    src = iw - d if i == 0 else iw + d
                    here = src >= 0 if i == 0 else src < n_w
                    p = piece(src, t, j * prow)

                    @pl.when(here & has[side])
                    def _():
                        rcopy(p, p, ag_s.at[i, d, c], ag_r.at[i, d, c], dev[side]).wait_send()


def local(latents, norm_gain, conv_weight, qkv_weight):
    n_t, n_h, n_w = (lax.axis_size(a) for a in ("ta", "ha", "wa"))
    t_dev, h_dev, w_dev, ch = latents.shape
    rows, cols_dev = h_dev // 2, w_dev // 2
    pd, head_dev, qkv_count, hd = qkv_weight.shape
    pc = n_w * cols_dev
    x = latents.astype(F32)
    rms = lax.rsqrt(jnp.mean(x * x, axis=-1, keepdims=True) + 1e-06)
    normed = jax.nn.silu(x * rms * norm_gain).astype(BF16)
    cols = jnp.stack([normed[:, :, 0], normed[:, :, w_dev - 1]])
    cw = conv_weight.reshape(3, 3, 3 * ch, ch)
    w2 = qkv_weight.reshape(pd, qkv_count * hd)
    frames = n_t * t_dev
    chunks = t_dev * (h_dev // CH)
    vm = pl.BlockSpec(memory_space=pltpu.VMEM)
    hbm = pl.BlockSpec(memory_space=pl.ANY)
    dma = pltpu.SemaphoreType.DMA
    block_out, att = pl.pallas_call(
        functools.partial(kernel, n_t, n_h, n_w),
        out_shape=(jax.ShapeDtypeStruct(latents.shape, BF16),
                   jax.ShapeDtypeStruct((frames, rows, pc, hd), BF16)),
        in_specs=[vm, vm, vm, hbm, hbm],
        out_specs=(vm, hbm),
        scratch_shapes=[
            pltpu.VMEM((t_dev + 2, h_dev + 2, w_dev, ch), BF16),
            pltpu.VMEM((2, t_dev + 2, 3 * h_dev, ch), BF16),
            pltpu.VMEM((2, t_dev + 2, 3 * h_dev, ch), F32),
            pltpu.VMEM((t_dev + 2, h_dev + 2, w_dev, 3 * ch), BF16),
            pltpu.VMEM((3, 3, 3 * ch, ch), BF16),
            pltpu.VMEM((n_t, pd, qkv_count * hd), BF16),
            pltpu.VMEM((ch // 128, CH * w_dev, 128), F32),
            pltpu.VMEM((n_w, t_dev, rows, cols_dev, pd), BF16),
            pltpu.VMEM((t_dev, n_t, rows, pc, hd), BF16),
            pltpu.VMEM((t_dev, rows + 2 * WIN, 2 * n_t, pc, hd), BF16),
            pltpu.VMEM((rows // WIN, WIN * pc, 3 * WIN * pc), F32),
            pltpu.VMEM((t_dev, n_t, rows, pc, hd), BF16),
            dma((2 + t_dev,)),
            dma((10,)), dma((10,)),
            dma((n_t,)), dma((n_t,)),
            dma((2, n_w, chunks)), dma((2, n_w, chunks)),
            dma((t_dev, 2)), dma((t_dev, 2)),
            dma((t_dev, n_t)), dma((t_dev, n_t)),
        ],
        compiler_params=pltpu.CompilerParams(
            collective_id=0, has_side_effects=True, vmem_limit_bytes=48 * 1024 * 1024),
    )(normed, cols, latents, cw, w2)
    return block_out, att.reshape(frames, rows, pc, head_dev, hd)


def solution(mesh):
    return jax.shard_map(
        local,
        mesh=mesh,
        in_specs=(P("ta", "ha", "wa", None), P(), P(), P(None, ("ta", "wa"), None, None)),
        out_specs=(P("ta", "ha", "wa", None), P(None, "ha", None, ("ta", "wa"), None)),
        check_vma=False,
    )
```

```python
import functools

import jax
import jax.numpy as jnp
from jax import lax
from jax.experimental import pallas as pl
from jax.experimental.pallas import tpu as pltpu
from jax.sharding import PartitionSpec as P

WIN = 4
CH = 8
MESH = pl.DeviceIdType.MESH
F32 = jnp.float32
BF16 = jnp.bfloat16


def kernel(n_t, n_h, n_w, latents, gain, cw_hbm, w_hbm, out_block, out_att,
           pad_n, edge_f, edge_b, pad_c, cf, x3, acc_buf, cw, wg, fbuf, pat, q_buf, kv, bias, o_buf,
           loc_sem, halo_s, halo_r, w_s, w_r, wf_s, wf_r, ag_s, ag_r, kv_s, kv_r, at_s, at_r):
    t_dev, h_dev, w_dev, ch = latents.shape
    rows = h_dev // 2
    cols_dev = w_dev // 2
    hd = q_buf.shape[-1]
    pd = pat.shape[-1]
    pc = n_w * cols_dev
    cpt = h_dev // CH
    prow = CH // 2
    it, ih, iw = lax.axis_index("ta"), lax.axis_index("ha"), lax.axis_index("wa")
    has = {"t-": it > 0, "t+": it < n_t - 1, "h-": ih > 0, "h+": ih < n_h - 1,
           "w-": iw > 0, "w+": iw < n_w - 1}
    opp = {"-": "+", "+": "-"}
    dev = {"t-": {"ta": it - 1}, "t+": {"ta": it + 1}, "h-": {"ha": ih - 1}, "h+": {"ha": ih + 1},
           "w-": {"wa": iw - 1}, "w+": {"wa": iw + 1}}

    def rcopy(src, dst, ss, rs, device):
        return pltpu.make_async_remote_copy(
            src_ref=src, dst_ref=dst, send_sem=ss, recv_sem=rs, device_id=device, device_id_type=MESH)

    cw_copy = pltpu.make_async_copy(cw_hbm, cw, loc_sem.at[0])
    cw_copy.start()
    own_w = pltpu.make_async_copy(w_hbm, wg.at[it], loc_sem.at[1])
    own_w.start()

    bar = pltpu.get_barrier_semaphore()
    count = jnp.int32(n_t - 1)
    for side in ("h-", "h+", "w-", "w+"):
        count = count + has[side].astype(jnp.int32)

        @pl.when(has[side])
        def _():
            pl.semaphore_signal(bar, inc=1, device_id=dev[side], device_id_type=MESH)
    for d in range(1, n_t):
        pl.semaphore_signal(bar, inc=1, device_id={"ta": lax.rem(it + d, n_t)}, device_id_type=MESH)

    @pl.loop(0, t_dev)
    def _(t):
        for r in range(h_dev):
            x = latents[t, r].astype(F32)
            ms = jnp.sum(x * x, axis=-1, keepdims=True) * (1.0 / ch)
            n = x * lax.rsqrt(ms + 1e-06) * gain[...]
            n = n / (1.0 + jnp.exp(-n))
            pad_n[t + 1, r + 1] = n.astype(BF16)
            edge_f[0, t, r:r + 1, :] = n[0:1]
            edge_f[1, t, r:r + 1, :] = n[w_dev - 1:w_dev]

    edge_b[...] = edge_f[...].astype(BF16)
    pl.semaphore_wait(bar, count)

    def halo(i, side, src, dst):
        c = rcopy(src, dst, halo_s.at[i], halo_r.at[i], dev[side])
        from_side = side[0] + opp[side[1]]

        def start():
            @pl.when(has[side])
            def _():
                c.start()

        def recv():
            @pl.when(has[from_side])
            def _():
                c.wait_recv()

        def sent():
            @pl.when(has[side])
            def _():
                c.wait_send()
        return start, recv, sent

    own = pl.ds(h_dev, h_dev)
    low = pl.ds(0, h_dev)
    high = pl.ds(2 * h_dev, h_dev)
    own_t = pl.ds(1, t_dev)
    own_h = pl.ds(1, h_dev)
    ph_w = [halo(0, "w-", edge_b.at[0], pad_c.at[1, own_t, own]),
            halo(1, "w+", edge_b.at[1], pad_c.at[0, own_t, own])]
    ph_t = {"t+": halo(2, "t-", pad_n.at[1, own_h], pad_n.at[t_dev + 1, own_h]),
            "t-": halo(3, "t+", pad_n.at[t_dev, own_h], pad_n.at[0, own_h])}
    ph_wt = {"t+": halo(4, "t-", pad_c.at[:, 1, own], pad_c.at[:, t_dev + 1, own]),
             "t-": halo(5, "t+", pad_c.at[:, t_dev, own], pad_c.at[:, 0, own])}

    def rows_cols(i, ts):
        return ([halo(i, "h-", pad_n.at[ts, 1], pad_n.at[ts, h_dev + 1]),
                 halo(i + 1, "h+", pad_n.at[ts, h_dev], pad_n.at[ts, 0])],
                [halo(i + 2, "h-", pad_c.at[:, ts, own], pad_c.at[:, ts, high]),
                 halo(i + 3, "h+", pad_c.at[:, ts, own], pad_c.at[:, ts, low])])

    hr_own, hc_own = rows_cols(6, own_t)
    ph_h = {"t-": rows_cols(10, pl.ds(0, 1)), "t+": rows_cols(14, pl.ds(t_dev + 1, 1))}
    for s in list(ph_t.values()) + ph_w + hr_own:
        s[0]()

    def zero(cond, ref, idx, shape):
        @pl.when(cond)
        def _():
            ref[idx] = jnp.zeros(shape, ref.dtype)

    no = {k: jnp.logical_not(v) for k, v in has.items()}
    full = slice(None)
    for side, s in (("w-", 0), ("w+", 1)):
        zero(no[side], pad_c, (s, own_t, own), (t_dev, h_dev, ch))
    for side, t in (("t-", 0), ("t+", t_dev + 1)):
        zero(no[side], pad_c, (full, t, own), (2, h_dev, ch))
        zero(no[side], pad_n, (t, own_h), (h_dev, w_dev, ch))
    for side, r, b in (("h-", 0, low), ("h+", h_dev + 1, high)):
        zero(no[side], pad_n, (full, r), (t_dev + 2, w_dev, ch))
        zero(no[side], pad_c, (full, full, b), (2, t_dev + 2, h_dev, ch))
        zero(no[side], kv, (full, pl.ds(0 if side == "h-" else rows + WIN, WIN)),
             (t_dev, WIN) + kv.shape[2:])

    for s in ph_w:
        s[1]()
    for s in list(ph_wt.values()) + hc_own:
        s[0]()

    edge = lax.broadcasted_iota(jnp.int32, (w_dev, ch), 0)

    def build(t, r):
        v16 = pad_n[t, r]
        v = v16.astype(F32)
        hr = pl.ds(h_dev - 1 + r, 1)
        left = jnp.where(edge == 0, cf[0, t, hr, :], pltpu.roll(v, 1, 0))
        right = jnp.where(edge == w_dev - 1, cf[1, t, hr, :], pltpu.roll(v, w_dev - 1, 0))
        x3[t, r, :, 0:ch] = left.astype(BF16)
        x3[t, r, :, ch:2 * ch] = v16
        x3[t, r, :, 2 * ch:3 * ch] = right.astype(BF16)

    cf[:, own_t, own] = pad_c[:, own_t, own].astype(F32)

    @pl.loop(1, t_dev + 1)
    def _(t):
        for r in range(1, h_dev + 1):
            build(t, r)

    for s in hr_own + hc_own:
        s[1]()
    for b in (low, high):
        cf[:, own_t, b] = pad_c[:, own_t, b].astype(F32)

    @pl.loop(1, t_dev + 1)
    def _(t):
        for r in (0, h_dev + 1):
            build(t, r)

    cw_copy.wait()

    def taps(acc, t, h0, frames):
        for a in frames:
            for b in range(3):
                acc = acc + jnp.dot(
                    x3[t + a, pl.ds(h0 + b, CH)].reshape(CH * w_dev, 3 * ch), cw[a, b],
                    preferred_element_type=F32)
        return acc

    for t in range(t_dev):
        @pl.loop(0, cpt)
        def _(j):
            acc = latents[t, pl.ds(j * CH, CH)].astype(F32).reshape(CH * w_dev, ch)
            acc_buf[t, j] = taps(acc, t, j * CH, [a for a in range(3) if 1 <= t + a <= t_dev])

    def halo_frame(side):
        ph_t[side][1]()
        ph_wt[side][1]()
        hs = ph_h[side][0] + ph_h[side][1]
        for s in hs:
            s[0]()
        f = 0 if side == "t-" else t_dev + 1
        cf[:, f, own] = pad_c[:, f, own].astype(F32)
        for r in range(1, h_dev + 1):
            build(f, r)
        for s in hs:
            s[1]()
        for b in (low, high):
            cf[:, f, b] = pad_c[:, f, b].astype(F32)
        for r in (0, h_dev + 1):
            build(f, r)

    def finish(t):
        @pl.loop(0, cpt)
        def _(j):
            h0 = j * CH
            blk = taps(acc_buf[t, j], t, h0, [a for a in range(3) if not 1 <= t + a <= t_dev])
            blk = blk.astype(BF16)
            out_block[t, pl.ds(h0, CH)] = blk.reshape(CH, w_dev, ch)
            blk = blk.astype(F32)
            for k in range(ch // 128):
                fbuf[k] = blk[:, k * 128:(k + 1) * 128]
            for k in range(ch // 128):
                for dw in range(2):
                    part = fbuf[k, pl.ds(dw, CH * cols_dev, stride=2), :].astype(BF16)
                    part = part.reshape(prow, 2, cols_dev, 128)
                    for dh in range(2):
                        lo = (dh * 2 + dw) * ch + k * 128
                        pat[iw, t, pl.ds(j * prow, prow), :, lo:lo + 128] = part[:, dh]

    def piece(src, t, i0):
        return pat.at[src, t, pl.ds(i0, prow)]

    sides = (("w+", 0), ("w-", 1))

    def send_own(t):
        for j in range(cpt):
            c = t * cpt + j
            p = piece(iw, t, j * prow)
            for side, i in sides:
                @pl.when(has[side])
                def _():
                    rcopy(p, p, ag_s.at[i, 0, c], ag_r.at[i, 0, c], dev[side]).start()

    def relay(t, d):
        for j in range(cpt):
            c = t * cpt + j
            for side, i in sides:
                src = iw - d if i == 0 else iw + d
                here = src >= 0 if i == 0 else src < n_w
                p = piece(src, t, j * prow)

                @pl.when(here)
                def _():
                    rcopy(p, p, ag_s.at[i, d - 1, c], ag_r.at[i, d - 1, c], dev[side]).wait_recv()
                    if d < n_w - 1:
                        @pl.when(has[side])
                        def _():
                            rcopy(p, p, ag_s.at[i, d, c], ag_r.at[i, d, c], dev[side]).start()

    pair = n_h % 2 == 0
    part_rows = pd // 2 if pair else pd
    mine = pl.ds((ih % 2) * part_rows, part_rows) if pair else pl.ds(0, pd)
    other = {"ha": ih + 1 - 2 * (ih % 2)}
    theirs = pl.ds((1 - ih % 2) * part_rows, part_rows) if pair else None

    def w_copy(d, src):
        return rcopy(w_hbm.at[:, mine], wg.at[src, :, mine], w_s.at[d], w_r.at[d],
                     {"ta": lax.rem(it + d, n_t)})

    def w_hand(d, part):
        src = lax.rem(it + n_t - d, n_t)
        return rcopy(wg.at[src, :, part], wg.at[src, :, part], wf_s.at[d], wf_r.at[d], other)

    def w_start():
        for d in range(1, n_t):
            w_copy(d, it).start()

    def w_mid():
        for d in range(1, n_t):
            w_copy(d, lax.rem(it + n_t - d, n_t)).wait_recv()
            if pair:
                w_hand(d, mine).start()

    def w_end():
        own_w.wait()
        if pair:
            for d in range(1, n_t):
                w_hand(d, theirs).wait_recv()

    def qkv(t):
        @pl.loop(0, n_t)
        def _(a):
            x = pat[:, t].reshape(n_w * rows * cols_dev, pd)
            w = jnp.concatenate([wg[a, s] for s in range(3)], axis=1)
            y = jnp.dot(x, w, preferred_element_type=F32).astype(BF16)
            y = y.reshape(n_w, rows, cols_dev, 3 * hd)
            for s in range(n_w):
                cc = pl.ds(s * cols_dev, cols_dev)
                q_buf[t, a, :, cc, :] = y[s, :, :, 0:hd]
                kv[t, pl.ds(WIN, rows), 2 * a, cc, :] = y[s, :, :, hd:2 * hd]
                kv[t, pl.ds(WIN, rows), 2 * a + 1, cc, :] = y[s, :, :, 2 * hd:3 * hd]

    def rim(t):
        return [halo_kv(t, 0, "h-", kv.at[t, pl.ds(WIN, WIN)], kv.at[t, pl.ds(rows + WIN, WIN)]),
                halo_kv(t, 1, "h+", kv.at[t, pl.ds(rows, WIN)], kv.at[t, pl.ds(0, WIN)])]

    def halo_kv(t, i, side, src, dst):
        c = rcopy(src, dst, kv_s.at[t, i], kv_r.at[t, i], dev[side])
        return has[side], has[side[0] + opp[side[1]]], c

    def rim_start(t):
        for out, _, c in rim(t):
            @pl.when(out)
            def _():
                c.start()

    def rim_recv(t):
        for _, inn, c in rim(t):
            @pl.when(inn)
            def _():
                c.wait_recv()

    scale = hd ** (-0.5) * 1.4426950408889634

    def attend(t, lo, hi):
        @pl.loop(lo, hi)
        def _(step):
            a = lax.rem(it + 1 + step, n_t)
            for b in range(rows // WIN):
                r = pl.ds(b * WIN, WIN)
                kr_ = pl.ds(b * WIN, 3 * WIN)
                q = q_buf[t, a, r].reshape(WIN * pc, hd)
                k = kv[t, kr_, 2 * a].reshape(3 * WIN * pc, hd)
                v = kv[t, kr_, 2 * a + 1].reshape(3 * WIN * pc, hd)
                s = lax.dot_general(q, k, (((1,), (1,)), ((), ())), preferred_element_type=F32)
                s = s + bias[b]
                m = jnp.max(s, axis=1, keepdims=True)
                e = jnp.exp2((s - m) * scale)
                z = jnp.sum(e, axis=1, keepdims=True)
                o = jnp.dot(e.astype(BF16), v, preferred_element_type=F32) / z
                o_buf[t, a, r] = o.astype(BF16).reshape(WIN, pc, hd)
            dst = out_att.at[it * t_dev + t]

            @pl.when(a != it)
            def _():
                rcopy(o_buf.at[t, a], dst, at_s.at[t, a], at_r.at[t, it], {"ta": a}).start()

            @pl.when(a == it)
            def _():
                pltpu.make_async_copy(o_buf.at[t, a], dst, loc_sem.at[2 + t]).start()

    halo_frame("t-")
    if t_dev == 1:
        halo_frame("t+")
    finish(0)
    send_own(0)
    for t in range(1, t_dev):
        if t == t_dev - 1:
            halo_frame("t+")
        finish(t)
    w_start()

    total_rows = rows * n_h
    bs = (WIN * pc, 3 * WIN * pc)
    qr = lax.broadcasted_iota(jnp.int32, bs, 0) // pc
    kr = lax.broadcasted_iota(jnp.int32, bs, 1) // pc - WIN
    for b in range(rows // WIN):
        kg = ih * rows + b * WIN + kr
        ok = (jnp.abs(qr - kr) <= WIN) & (kg >= 0) & (kg < total_rows)
        bias[b] = jnp.where(ok, 0.0, -1e30).astype(F32)

    for d in range(1, n_w - 1):
        relay(0, d)
    if t_dev > 1:
        send_own(1)
    w_mid()
    if n_w > 1:
        relay(0, n_w - 1)
    w_end()
    for t in range(t_dev):
        more = t + 1 < t_dev
        qkv(t)
        rim_start(t)
        steps = n_w - 2
        rim_done = False
        for d in range(1, n_w - 1):
            if more:
                relay(t + 1, d)
            if not rim_done:
                rim_recv(t)
                rim_done = True
            attend(t, n_t * (d - 1) // steps, n_t * d // steps)
        if not rim_done:
            rim_recv(t)
            attend(t, 0, n_t)
        if more:
            if t + 2 < t_dev:
                send_own(t + 2)
            if n_w > 1:
                relay(t + 1, n_w - 1)

    for t in range(t_dev):
        pltpu.make_async_copy(o_buf.at[t, it], out_att.at[it * t_dev + t], loc_sem.at[2 + t]).wait()
        for d in range(1, n_t):
            src = lax.rem(it + d, n_t)
            rcopy(o_buf.at[t, src], out_att.at[src * t_dev + t], at_s.at[t, src], at_r.at[t, src],
                  {"ta": src}).wait()
        for out, _, c in rim(t):
            @pl.when(out)
            def _():
                c.wait_send()
    for s in (ph_w + list(ph_t.values()) + list(ph_wt.values()) + hr_own + hc_own
              + ph_h["t-"][0] + ph_h["t-"][1] + ph_h["t+"][0] + ph_h["t+"][1]):
        s[2]()
    for d in range(1, n_t):
        w_copy(d, it).wait_send()
        if pair:
            w_hand(d, mine).wait_send()
    for t in range(t_dev):
        for j in range(cpt):
            c = t * cpt + j
            for side, i in sides:
                for d in range(n_w - 1):
                    src = iw - d if i == 0 else iw + d
                    here = src >= 0 if i == 0 else src < n_w
                    p = piece(src, t, j * prow)

                    @pl.when(here & has[side])
                    def _():
                        rcopy(p, p, ag_s.at[i, d, c], ag_r.at[i, d, c], dev[side]).wait_send()


def local(latents, norm_gain, conv_weight, qkv_weight):
    n_t, n_h, n_w = (lax.axis_size(a) for a in ("ta", "ha", "wa"))
    t_dev, h_dev, w_dev, ch = latents.shape
    rows, cols_dev = h_dev // 2, w_dev // 2
    pd, head_dev, qkv_count, hd = qkv_weight.shape
    pc = n_w * cols_dev
    cw = conv_weight.reshape(3, 3, 3 * ch, ch)
    w2 = qkv_weight.transpose(1, 2, 0, 3).reshape(qkv_count, pd, hd)
    frames = n_t * t_dev
    chunks = t_dev * (h_dev // CH)
    vm = pl.BlockSpec(memory_space=pltpu.VMEM)
    hbm = pl.BlockSpec(memory_space=pl.ANY)
    dma = pltpu.SemaphoreType.DMA
    block_out, att = pl.pallas_call(
        functools.partial(kernel, n_t, n_h, n_w),
        out_shape=(jax.ShapeDtypeStruct(latents.shape, BF16),
                   jax.ShapeDtypeStruct((frames, rows, pc, hd), BF16)),
        in_specs=[vm, vm, hbm, hbm],
        out_specs=(vm, hbm),
        scratch_shapes=[
            pltpu.VMEM((t_dev + 2, h_dev + 2, w_dev, ch), BF16),
            pltpu.VMEM((2, t_dev, h_dev, ch), F32),
            pltpu.VMEM((2, t_dev, h_dev, ch), BF16),
            pltpu.VMEM((2, t_dev + 2, 3 * h_dev, ch), BF16),
            pltpu.VMEM((2, t_dev + 2, 3 * h_dev, ch), F32),
            pltpu.VMEM((t_dev + 2, h_dev + 2, w_dev, 3 * ch), BF16),
            pltpu.VMEM((t_dev, h_dev // CH, CH * w_dev, ch), F32),
            pltpu.VMEM((3, 3, 3 * ch, ch), BF16),
            pltpu.VMEM((n_t, qkv_count, pd, hd), BF16),
            pltpu.VMEM((ch // 128, CH * w_dev, 128), F32),
            pltpu.VMEM((n_w, t_dev, rows, cols_dev, pd), BF16),
            pltpu.VMEM((t_dev, n_t, rows, pc, hd), BF16),
            pltpu.VMEM((t_dev, rows + 2 * WIN, 2 * n_t, pc, hd), BF16),
            pltpu.VMEM((rows // WIN, WIN * pc, 3 * WIN * pc), F32),
            pltpu.VMEM((t_dev, n_t, rows, pc, hd), BF16),
            dma((2 + t_dev,)),
            dma((18,)), dma((18,)),
            dma((n_t,)), dma((n_t,)),
            dma((n_t,)), dma((n_t,)),
            dma((2, n_w, chunks)), dma((2, n_w, chunks)),
            dma((t_dev, 2)), dma((t_dev, 2)),
            dma((t_dev, n_t)), dma((t_dev, n_t)),
        ],
        compiler_params=pltpu.CompilerParams(
            collective_id=0, has_side_effects=True, vmem_limit_bytes=48 * 1024 * 1024),
    )(latents, norm_gain.reshape(1, ch), cw, w2)
    return block_out, att.reshape(frames, rows, pc, head_dev, hd)


def solution(mesh):
    return jax.shard_map(
        local,
        mesh=mesh,
        in_specs=(P("ta", "ha", "wa", None), P(), P(), P(None, ("ta", "wa"), None, None)),
        out_specs=(P("ta", "ha", "wa", None), P(None, "ha", None, ("ta", "wa"), None)),
        check_vma=False,
    )
```

```python
import functools

import jax
import jax.numpy as jnp
from jax import lax
from jax.experimental import pallas as pl
from jax.experimental.pallas import tpu as pltpu
from jax.sharding import PartitionSpec as P

WIN = 4
CH = 8
MESH = pl.DeviceIdType.MESH
F32 = jnp.float32
BF16 = jnp.bfloat16


def kernel(n_t, n_h, n_w, latents, gain, cw_hbm, w_hbm, out_block, out_att,
           pad_n, edge_f, edge_b, pad_c, cf, x3, acc_buf, cw, wg, fbuf, pat, q_buf, kv, bias, o_buf,
           loc_sem, halo_s, halo_r, w_s, w_r, wf_s, wf_r, ag_s, ag_r, kv_s, kv_r, at_s, at_r):
    t_dev, h_dev, w_dev, ch = latents.shape
    rows = h_dev // 2
    cols_dev = w_dev // 2
    hd = q_buf.shape[-1]
    pd = pat.shape[-1]
    pc = n_w * cols_dev
    cpt = h_dev // CH
    prow = CH // 2
    it, ih, iw = lax.axis_index("ta"), lax.axis_index("ha"), lax.axis_index("wa")
    has = {"t-": it > 0, "t+": it < n_t - 1, "h-": ih > 0, "h+": ih < n_h - 1,
           "w-": iw > 0, "w+": iw < n_w - 1}
    opp = {"-": "+", "+": "-"}
    dev = {"t-": {"ta": it - 1}, "t+": {"ta": it + 1}, "h-": {"ha": ih - 1}, "h+": {"ha": ih + 1},
           "w-": {"wa": iw - 1}, "w+": {"wa": iw + 1}}

    def rcopy(src, dst, ss, rs, device):
        return pltpu.make_async_remote_copy(
            src_ref=src, dst_ref=dst, send_sem=ss, recv_sem=rs, device_id=device, device_id_type=MESH)

    cw_copy = pltpu.make_async_copy(cw_hbm, cw, loc_sem.at[0])
    cw_copy.start()
    own_w = pltpu.make_async_copy(w_hbm, wg.at[it], loc_sem.at[1])
    own_w.start()

    bar = pltpu.get_barrier_semaphore()
    count = jnp.int32(n_t - 1)
    for side in ("h-", "h+", "w-", "w+"):
        count = count + has[side].astype(jnp.int32)

        @pl.when(has[side])
        def _():
            pl.semaphore_signal(bar, inc=1, device_id=dev[side], device_id_type=MESH)
    for d in range(1, n_t):
        pl.semaphore_signal(bar, inc=1, device_id={"ta": lax.rem(it + d, n_t)}, device_id_type=MESH)

    @pl.loop(0, t_dev)
    def _(t):
        for r in range(h_dev):
            x = latents[t, r].astype(F32)
            ms = jnp.sum(x * x, axis=-1, keepdims=True) * (1.0 / ch)
            n = x * lax.rsqrt(ms + 1e-06) * gain[...]
            n = n / (1.0 + jnp.exp(-n))
            pad_n[t + 1, r + 1] = n.astype(BF16)
            edge_f[0, t, r:r + 1, :] = n[0:1]
            edge_f[1, t, r:r + 1, :] = n[w_dev - 1:w_dev]

    edge_b[...] = edge_f[...].astype(BF16)
    pl.semaphore_wait(bar, count)

    def halo(i, side, src, dst):
        c = rcopy(src, dst, halo_s.at[i], halo_r.at[i], dev[side])
        from_side = side[0] + opp[side[1]]

        def start():
            @pl.when(has[side])
            def _():
                c.start()

        def recv():
            @pl.when(has[from_side])
            def _():
                c.wait_recv()

        def sent():
            @pl.when(has[side])
            def _():
                c.wait_send()
        return start, recv, sent

    own = pl.ds(h_dev, h_dev)
    low = pl.ds(0, h_dev)
    high = pl.ds(2 * h_dev, h_dev)
    own_t = pl.ds(1, t_dev)
    own_h = pl.ds(1, h_dev)
    ph_w = [halo(0, "w-", edge_b.at[0], pad_c.at[1, own_t, own]),
            halo(1, "w+", edge_b.at[1], pad_c.at[0, own_t, own])]
    ph_t = {"t+": halo(2, "t-", pad_n.at[1, own_h], pad_n.at[t_dev + 1, own_h]),
            "t-": halo(3, "t+", pad_n.at[t_dev, own_h], pad_n.at[0, own_h])}
    ph_wt = {"t+": halo(4, "t-", pad_c.at[:, 1, own], pad_c.at[:, t_dev + 1, own]),
             "t-": halo(5, "t+", pad_c.at[:, t_dev, own], pad_c.at[:, 0, own])}

    def rows_cols(i, ts):
        return ([halo(i, "h-", pad_n.at[ts, 1], pad_n.at[ts, h_dev + 1]),
                 halo(i + 1, "h+", pad_n.at[ts, h_dev], pad_n.at[ts, 0])],
                [halo(i + 2, "h-", pad_c.at[:, ts, own], pad_c.at[:, ts, high]),
                 halo(i + 3, "h+", pad_c.at[:, ts, own], pad_c.at[:, ts, low])])

    hr_own, hc_own = rows_cols(6, own_t)
    ph_h = {"t-": rows_cols(10, pl.ds(0, 1)), "t+": rows_cols(14, pl.ds(t_dev + 1, 1))}
    for s in [ph_t["t-"]] + ph_w + hr_own:
        s[0]()

    def zero(cond, ref, idx, shape):
        @pl.when(cond)
        def _():
            ref[idx] = jnp.zeros(shape, ref.dtype)

    no = {k: jnp.logical_not(v) for k, v in has.items()}
    full = slice(None)
    for side, s in (("w-", 0), ("w+", 1)):
        zero(no[side], pad_c, (s, own_t, own), (t_dev, h_dev, ch))
    for side, t in (("t-", 0), ("t+", t_dev + 1)):
        zero(no[side], pad_c, (full, t, own), (2, h_dev, ch))
        zero(no[side], pad_n, (t, own_h), (h_dev, w_dev, ch))
    for side, r, b in (("h-", 0, low), ("h+", h_dev + 1, high)):
        zero(no[side], pad_n, (full, r), (t_dev + 2, w_dev, ch))
        zero(no[side], pad_c, (full, full, b), (2, t_dev + 2, h_dev, ch))
        zero(no[side], kv, (full, pl.ds(0 if side == "h-" else rows + WIN, WIN)),
             (t_dev, WIN) + kv.shape[2:])

    for s in ph_w:
        s[1]()
    for s in list(ph_wt.values()) + hc_own:
        s[0]()

    edge = lax.broadcasted_iota(jnp.int32, (w_dev, ch), 0)

    def build(t, r):
        v16 = pad_n[t, r]
        v = v16.astype(F32)
        hr = pl.ds(h_dev - 1 + r, 1)
        left = jnp.where(edge == 0, cf[0, t, hr, :], pltpu.roll(v, 1, 0))
        right = jnp.where(edge == w_dev - 1, cf[1, t, hr, :], pltpu.roll(v, w_dev - 1, 0))
        x3[t, r, :, 0:ch] = left.astype(BF16)
        x3[t, r, :, ch:2 * ch] = v16
        x3[t, r, :, 2 * ch:3 * ch] = right.astype(BF16)

    cf[:, own_t, own] = pad_c[:, own_t, own].astype(F32)

    @pl.loop(1, t_dev + 1)
    def _(t):
        for r in range(1, h_dev + 1):
            build(t, r)

    for s in hr_own + hc_own:
        s[1]()
    for b in (low, high):
        cf[:, own_t, b] = pad_c[:, own_t, b].astype(F32)

    @pl.loop(1, t_dev + 1)
    def _(t):
        for r in (0, h_dev + 1):
            build(t, r)

    cw_copy.wait()

    def taps(acc, t, h0, frames):
        for a in frames:
            for b in range(3):
                acc = acc + jnp.dot(
                    x3[t + a, pl.ds(h0 + b, CH)].reshape(CH * w_dev, 3 * ch), cw[a, b],
                    preferred_element_type=F32)
        return acc

    for t in range(t_dev):
        @pl.loop(0, cpt)
        def _(j):
            acc = latents[t, pl.ds(j * CH, CH)].astype(F32).reshape(CH * w_dev, ch)
            acc_buf[t, j] = taps(acc, t, j * CH, [a for a in range(3) if 1 <= t + a <= t_dev])

    def halo_frame(side):
        if side == "t+":
            ph_t[side][1]()
        ph_wt[side][1]()
        hs = ph_h[side][0] + ph_h[side][1]
        for s in hs:
            s[0]()
        f = 0 if side == "t-" else t_dev + 1
        cf[:, f, own] = pad_c[:, f, own].astype(F32)
        for r in range(1, h_dev + 1):
            build(f, r)
        for s in hs:
            s[1]()
        for b in (low, high):
            cf[:, f, b] = pad_c[:, f, b].astype(F32)
        for r in (0, h_dev + 1):
            build(f, r)

    def finish(t):
        for j in range(cpt):
            h0 = j * CH
            blk = taps(acc_buf[t, j], t, h0, [a for a in range(3) if not 1 <= t + a <= t_dev])
            blk = blk.astype(BF16)
            out_block[t, pl.ds(h0, CH)] = blk.reshape(CH, w_dev, ch)
            blk = blk.astype(F32)
            for k in range(ch // 128):
                fbuf[k] = blk[:, k * 128:(k + 1) * 128]
            for k in range(ch // 128):
                for dw in range(2):
                    part = fbuf[k, pl.ds(dw, CH * cols_dev, stride=2), :].astype(BF16)
                    part = part.reshape(prow, 2, cols_dev, 128)
                    for dh in range(2):
                        lo = (dh * 2 + dw) * ch + k * 128
                        pat[iw, t, pl.ds(j * prow, prow), :, lo:lo + 128] = part[:, dh]
            if t == 0:
                send_own(0, j)

    def piece(src, t, i0):
        return pat.at[src, t, pl.ds(i0, prow)]

    sides = (("w+", 0), ("w-", 1))

    def send_own(t, only=None):
        for j in range(cpt) if only is None else (only,):
            c = t * cpt + j
            p = piece(iw, t, j * prow)
            for side, i in sides:
                @pl.when(has[side])
                def _():
                    rcopy(p, p, ag_s.at[i, 0, c], ag_r.at[i, 0, c], dev[side]).start()

    def relay(t, d):
        for j in range(cpt):
            c = t * cpt + j
            for side, i in sides:
                src = iw - d if i == 0 else iw + d
                here = src >= 0 if i == 0 else src < n_w
                p = piece(src, t, j * prow)

                @pl.when(here)
                def _():
                    rcopy(p, p, ag_s.at[i, d - 1, c], ag_r.at[i, d - 1, c], dev[side]).wait_recv()
                    if d < n_w - 1:
                        @pl.when(has[side])
                        def _():
                            rcopy(p, p, ag_s.at[i, d, c], ag_r.at[i, d, c], dev[side]).start()

    pair = n_h % 2 == 0
    part_rows = pd // 2 if pair else pd
    mine = pl.ds((ih % 2) * part_rows, part_rows) if pair else pl.ds(0, pd)
    other = {"ha": ih + 1 - 2 * (ih % 2)}
    theirs = pl.ds((1 - ih % 2) * part_rows, part_rows) if pair else None

    def w_copy(d, src):
        return rcopy(w_hbm.at[:, mine], wg.at[src, :, mine], w_s.at[d], w_r.at[d],
                     {"ta": lax.rem(it + d, n_t)})

    def w_hand(d, part):
        src = lax.rem(it + n_t - d, n_t)
        return rcopy(wg.at[src, :, part], wg.at[src, :, part], wf_s.at[d], wf_r.at[d], other)

    def w_start():
        for d in range(1, n_t):
            w_copy(d, it).start()

    def w_mid():
        for d in range(1, n_t):
            w_copy(d, lax.rem(it + n_t - d, n_t)).wait_recv()
            if pair:
                w_hand(d, mine).start()

    def w_end():
        own_w.wait()
        if pair:
            for d in range(1, n_t):
                w_hand(d, theirs).wait_recv()

    def head_at(step):
        return lax.rem(it + 1 + step, n_t)

    def rim(t, a):
        lo, hi, two = pl.ds(WIN, WIN), pl.ds(rows, WIN), pl.ds(2 * a, 2)
        return [halo_kv(t, 0, a, "h-", kv.at[t, lo, two], kv.at[t, pl.ds(rows + WIN, WIN), two]),
                halo_kv(t, 1, a, "h+", kv.at[t, hi, two], kv.at[t, pl.ds(0, WIN), two])]

    def halo_kv(t, i, a, side, src, dst):
        c = rcopy(src, dst, kv_s.at[t, i, a], kv_r.at[t, i, a], dev[side])
        return has[side], has[side[0] + opp[side[1]]], c

    def qkv(t, step):
        a = head_at(step)
        x = pat[:, t].reshape(n_w * rows * cols_dev, pd)
        w = jnp.concatenate([wg[a, s] for s in range(3)], axis=1)
        y = jnp.dot(x, w, preferred_element_type=F32).astype(BF16)
        y = y.reshape(n_w, rows, cols_dev, 3 * hd)
        for s in range(n_w):
            cc = pl.ds(s * cols_dev, cols_dev)
            q_buf[t, a, :, cc, :] = y[s, :, :, 0:hd]
            kv[t, pl.ds(WIN, rows), 2 * a, cc, :] = y[s, :, :, hd:2 * hd]
            kv[t, pl.ds(WIN, rows), 2 * a + 1, cc, :] = y[s, :, :, 2 * hd:3 * hd]
        for out, _, c in rim(t, a):
            @pl.when(out)
            def _():
                c.start()

    scale = hd ** (-0.5) * 1.4426950408889634

    def attend(t, step):
        a = head_at(step)
        for _, inn, c in rim(t, a):
            @pl.when(inn)
            def _():
                c.wait_recv()
        for b in range(rows // WIN):
            r = pl.ds(b * WIN, WIN)
            kr_ = pl.ds(b * WIN, 3 * WIN)
            q = q_buf[t, a, r].reshape(WIN * pc, hd)
            k = kv[t, kr_, 2 * a].reshape(3 * WIN * pc, hd)
            v = kv[t, kr_, 2 * a + 1].reshape(3 * WIN * pc, hd)
            s = lax.dot_general(q, k, (((1,), (1,)), ((), ())), preferred_element_type=F32)
            s = s + bias[b]
            m = jnp.max(s, axis=1, keepdims=True)
            e = jnp.exp2((s - m) * scale)
            z = jnp.sum(e, axis=1, keepdims=True)
            o = jnp.dot(e.astype(BF16), v, preferred_element_type=F32) / z
            o_buf[t, a, r] = o.astype(BF16).reshape(WIN, pc, hd)
        dst = out_att.at[it * t_dev + t]

        @pl.when(a != it)
        def _():
            rcopy(o_buf.at[t, a], dst, at_s.at[t, a], at_r.at[t, it], {"ta": a}).start()

        @pl.when(a == it)
        def _():
            pltpu.make_async_copy(o_buf.at[t, a], dst, loc_sem.at[2 + t]).start()

    ph_t["t-"][1]()
    ph_t["t+"][0]()
    w_start()

    halo_frame("t-")
    if t_dev == 1:
        halo_frame("t+")
    finish(0)
    for t in range(1, t_dev):
        if t == t_dev - 1:
            halo_frame("t+")
        finish(t)

    total_rows = rows * n_h
    bs = (WIN * pc, 3 * WIN * pc)
    qr = lax.broadcasted_iota(jnp.int32, bs, 0) // pc
    kr = lax.broadcasted_iota(jnp.int32, bs, 1) // pc - WIN
    for b in range(rows // WIN):
        kg = ih * rows + b * WIN + kr
        ok = (jnp.abs(qr - kr) <= WIN) & (kg >= 0) & (kg < total_rows)
        bias[b] = jnp.where(ok, 0.0, -1e30).astype(F32)

    for d in range(1, n_w - 1):
        relay(0, d)
    if t_dev > 1:
        send_own(1)
    w_mid()
    if n_w > 1:
        relay(0, n_w - 1)
    w_end()
    for t in range(t_dev):
        more = t + 1 < t_dev
        if more:
            @pl.loop(0, n_t)
            def _(step):
                qkv(t, step)
            steps = max(n_w - 2, 1)
            for d in range(1, steps + 1):
                if d < n_w - 1:
                    relay(t + 1, d)

                @pl.loop(n_t * (d - 1) // steps, n_t * d // steps)
                def _(step):
                    attend(t, step)
        else:
            qkv(t, 0)

            @pl.loop(0, n_t - 1)
            def _(step):
                qkv(t, step + 1)
                attend(t, step)
            attend(t, n_t - 1)
        if more:
            if t + 2 < t_dev:
                send_own(t + 2)
            if n_w > 1:
                relay(t + 1, n_w - 1)

    for t in range(t_dev):
        pltpu.make_async_copy(o_buf.at[t, it], out_att.at[it * t_dev + t], loc_sem.at[2 + t]).wait()
        for d in range(1, n_t):
            src = lax.rem(it + d, n_t)
            rcopy(o_buf.at[t, src], out_att.at[src * t_dev + t], at_s.at[t, src], at_r.at[t, src],
                  {"ta": src}).wait()
        for a in range(n_t):
            for out, _, c in rim(t, a):
                @pl.when(out)
                def _():
                    c.wait_send()
    for s in (ph_w + list(ph_t.values()) + list(ph_wt.values()) + hr_own + hc_own
              + ph_h["t-"][0] + ph_h["t-"][1] + ph_h["t+"][0] + ph_h["t+"][1]):
        s[2]()
    for d in range(1, n_t):
        w_copy(d, it).wait_send()
        if pair:
            w_hand(d, mine).wait_send()
    for t in range(t_dev):
        for j in range(cpt):
            c = t * cpt + j
            for side, i in sides:
                for d in range(n_w - 1):
                    src = iw - d if i == 0 else iw + d
                    here = src >= 0 if i == 0 else src < n_w
                    p = piece(src, t, j * prow)

                    @pl.when(here & has[side])
                    def _():
                        rcopy(p, p, ag_s.at[i, d, c], ag_r.at[i, d, c], dev[side]).wait_send()


def local(latents, norm_gain, conv_weight, qkv_weight):
    n_t, n_h, n_w = (lax.axis_size(a) for a in ("ta", "ha", "wa"))
    t_dev, h_dev, w_dev, ch = latents.shape
    rows, cols_dev = h_dev // 2, w_dev // 2
    pd, head_dev, qkv_count, hd = qkv_weight.shape
    pc = n_w * cols_dev
    cw = conv_weight.reshape(3, 3, 3 * ch, ch)
    w2 = qkv_weight.transpose(1, 2, 0, 3).reshape(qkv_count, pd, hd)
    frames = n_t * t_dev
    chunks = t_dev * (h_dev // CH)
    vm = pl.BlockSpec(memory_space=pltpu.VMEM)
    hbm = pl.BlockSpec(memory_space=pl.ANY)
    dma = pltpu.SemaphoreType.DMA
    block_out, att = pl.pallas_call(
        functools.partial(kernel, n_t, n_h, n_w),
        out_shape=(jax.ShapeDtypeStruct(latents.shape, BF16),
                   jax.ShapeDtypeStruct((frames, rows, pc, hd), BF16)),
        in_specs=[vm, vm, hbm, hbm],
        out_specs=(vm, hbm),
        scratch_shapes=[
            pltpu.VMEM((t_dev + 2, h_dev + 2, w_dev, ch), BF16),
            pltpu.VMEM((2, t_dev, h_dev, ch), F32),
            pltpu.VMEM((2, t_dev, h_dev, ch), BF16),
            pltpu.VMEM((2, t_dev + 2, 3 * h_dev, ch), BF16),
            pltpu.VMEM((2, t_dev + 2, 3 * h_dev, ch), F32),
            pltpu.VMEM((t_dev + 2, h_dev + 2, w_dev, 3 * ch), BF16),
            pltpu.VMEM((t_dev, h_dev // CH, CH * w_dev, ch), F32),
            pltpu.VMEM((3, 3, 3 * ch, ch), BF16),
            pltpu.VMEM((n_t, qkv_count, pd, hd), BF16),
            pltpu.VMEM((ch // 128, CH * w_dev, 128), F32),
            pltpu.VMEM((n_w, t_dev, rows, cols_dev, pd), BF16),
            pltpu.VMEM((t_dev, n_t, rows, pc, hd), BF16),
            pltpu.VMEM((t_dev, rows + 2 * WIN, 2 * n_t, pc, hd), BF16),
            pltpu.VMEM((rows // WIN, WIN * pc, 3 * WIN * pc), F32),
            pltpu.VMEM((t_dev, n_t, rows, pc, hd), BF16),
            dma((2 + t_dev,)),
            dma((18,)), dma((18,)),
            dma((n_t,)), dma((n_t,)),
            dma((n_t,)), dma((n_t,)),
            dma((2, n_w, chunks)), dma((2, n_w, chunks)),
            dma((t_dev, 2, n_t)), dma((t_dev, 2, n_t)),
            dma((t_dev, n_t)), dma((t_dev, n_t)),
        ],
        compiler_params=pltpu.CompilerParams(
            collective_id=0, has_side_effects=True, vmem_limit_bytes=60 * 1024 * 1024),
    )(latents, norm_gain.reshape(1, ch), cw, w2)
    return block_out, att.reshape(frames, rows, pc, head_dev, hd)


def solution(mesh):
    return jax.shard_map(
        local,
        mesh=mesh,
        in_specs=(P("ta", "ha", "wa", None), P(), P(), P(None, ("ta", "wa"), None, None)),
        out_specs=(P("ta", "ha", "wa", None), P(None, "ha", None, ("ta", "wa"), None)),
        check_vma=False,
    )
```

```python
import functools

import jax
import jax.numpy as jnp
from jax import lax
from jax.experimental import pallas as pl
from jax.experimental.pallas import tpu as pltpu
from jax.sharding import PartitionSpec as P

WIN = 4
CH = 8
MESH = pl.DeviceIdType.MESH
F32 = jnp.float32
BF16 = jnp.bfloat16


def kernel(n_t, n_h, n_w, lat_hbm, gain_hbm, cw_hbm, w_hbm, blk_hbm, out_att,
           out_block, latents, gain, raw, pad_n, edge_f, edge_b, pad_c, cf, x3, acc_buf, cw, wg, fbuf, pat, q_buf, kv, bias, o_buf,
           loc_sem, halo_s, halo_r, w_s, w_r, wf_s, wf_r, ag_s, ag_r, kv_s, kv_r, at_s, at_r):
    t_dev, h_dev, w_dev, ch = latents.shape
    rows = h_dev // 2
    cols_dev = w_dev // 2
    hd = q_buf.shape[-1]
    pd = pat.shape[-1]
    pc = n_w * cols_dev
    cpt = h_dev // CH
    prow = CH // 2
    it, ih, iw = lax.axis_index("ta"), lax.axis_index("ha"), lax.axis_index("wa")
    has = {"t-": it > 0, "t+": it < n_t - 1, "h-": ih > 0, "h+": ih < n_h - 1,
           "w-": iw > 0, "w+": iw < n_w - 1}
    opp = {"-": "+", "+": "-"}
    dev = {"t-": {"ta": it - 1}, "t+": {"ta": it + 1}, "h-": {"ha": ih - 1}, "h+": {"ha": ih + 1},
           "w-": {"wa": iw - 1}, "w+": {"wa": iw + 1}}

    def rcopy(src, dst, ss, rs, device):
        return pltpu.make_async_remote_copy(
            src_ref=src, dst_ref=dst, send_sem=ss, recv_sem=rs, device_id=device, device_id_type=MESH)

    lat_copy = pltpu.make_async_copy(lat_hbm, latents, loc_sem.at[2 + t_dev])
    lat_copy.start()
    gain_copy = pltpu.make_async_copy(gain_hbm, gain, loc_sem.at[3 + t_dev])
    gain_copy.start()
    cw_copy = pltpu.make_async_copy(cw_hbm, cw, loc_sem.at[0])
    cw_copy.start()
    own_w = pltpu.make_async_copy(w_hbm, wg.at[it], loc_sem.at[1])
    own_w.start()

    bar = pltpu.get_barrier_semaphore()
    count = jnp.int32(n_t - 1)
    for side in ("h-", "h+", "w-", "w+"):
        count = count + has[side].astype(jnp.int32)

        @pl.when(has[side])
        def _():
            pl.semaphore_signal(bar, inc=1, device_id=dev[side], device_id_type=MESH)
    for d in range(1, n_t):
        pl.semaphore_signal(bar, inc=1, device_id={"ta": lax.rem(it + d, n_t)}, device_id_type=MESH)

    pl.semaphore_wait(bar, count)

    def halo(i, side, src, dst):
        c = rcopy(src, dst, halo_s.at[i], halo_r.at[i], dev[side])
        from_side = side[0] + opp[side[1]]

        def start():
            @pl.when(has[side])
            def _():
                c.start()

        def recv():
            @pl.when(has[from_side])
            def _():
                c.wait_recv()

        def sent():
            @pl.when(has[side])
            def _():
                c.wait_send()
        return start, recv, sent

    own = pl.ds(h_dev, h_dev)
    low = pl.ds(0, h_dev)
    high = pl.ds(2 * h_dev, h_dev)
    own_t = pl.ds(1, t_dev)
    own_h = pl.ds(1, h_dev)
    ph_w = [halo(0, "w-", edge_b.at[0], pad_c.at[1, own_t, own]),
            halo(1, "w+", edge_b.at[1], pad_c.at[0, own_t, own])]
    ph_t = {"t+": halo(2, "t-", lat_hbm.at[0], raw.at[1]),
            "t-": halo(3, "t+", lat_hbm.at[t_dev - 1], raw.at[0])}
    ph_wt = {"t+": halo(4, "t-", pad_c.at[:, 1, own], pad_c.at[:, t_dev + 1, own]),
             "t-": halo(5, "t+", pad_c.at[:, t_dev, own], pad_c.at[:, 0, own])}

    def rows_cols(i, ts):
        return ([halo(i, "h-", pad_n.at[ts, 1], pad_n.at[ts, h_dev + 1]),
                 halo(i + 1, "h+", pad_n.at[ts, h_dev], pad_n.at[ts, 0])],
                [halo(i + 2, "h-", pad_c.at[:, ts, own], pad_c.at[:, ts, high]),
                 halo(i + 3, "h+", pad_c.at[:, ts, own], pad_c.at[:, ts, low])])

    hr_own, hc_own = rows_cols(6, own_t)
    ph_h = {"t-": rows_cols(10, pl.ds(0, 1)), "t+": rows_cols(14, pl.ds(t_dev + 1, 1))}
    ph_t["t-"][0]()

    def norm(x16):
        x = x16.astype(F32)
        ms = jnp.sum(x * x, axis=-1, keepdims=True) * (1.0 / ch)
        n = x * lax.rsqrt(ms + 1e-06) * half_gain
        return n * jnp.tanh(n) + n

    lat_copy.wait()
    gain_copy.wait()
    half_gain = gain[...] * 0.5

    @pl.loop(0, t_dev)
    def _(t):
        for r in range(h_dev):
            n = norm(latents[t, r])
            pad_n[t + 1, r + 1] = n.astype(BF16)
            edge_f[0, t, r:r + 1, :] = n[0:1]
            edge_f[1, t, r:r + 1, :] = n[w_dev - 1:w_dev]

    edge_b[...] = edge_f[...].astype(BF16)
    for s in ph_w + hr_own:
        s[0]()

    def zero(cond, ref, idx, shape):
        @pl.when(cond)
        def _():
            ref[idx] = jnp.zeros(shape, ref.dtype)

    no = {k: jnp.logical_not(v) for k, v in has.items()}
    full = slice(None)
    for side, s in (("w-", 0), ("w+", 1)):
        zero(no[side], pad_c, (s, own_t, own), (t_dev, h_dev, ch))
    for side, t in (("t-", 0), ("t+", t_dev + 1)):
        zero(no[side], pad_c, (full, t, own), (2, h_dev, ch))
        zero(no[side], raw, (0 if t == 0 else 1,), (h_dev, w_dev, ch))
    for side, r, b in (("h-", 0, low), ("h+", h_dev + 1, high)):
        zero(no[side], pad_n, (full, r), (t_dev + 2, w_dev, ch))
        zero(no[side], pad_c, (full, full, b), (2, t_dev + 2, h_dev, ch))
        zero(no[side], kv, (full, pl.ds(0 if side == "h-" else rows + WIN, WIN)),
             (t_dev, WIN) + kv.shape[2:])

    for s in ph_w:
        s[1]()
    for s in list(ph_wt.values()) + hc_own:
        s[0]()

    edge = lax.broadcasted_iota(jnp.int32, (w_dev, ch), 0)

    def build(t, r):
        v16 = pad_n[t, r]
        v = v16.astype(F32)
        hr = pl.ds(h_dev - 1 + r, 1)
        left = jnp.where(edge == 0, cf[0, t, hr, :], pltpu.roll(v, 1, 0))
        right = jnp.where(edge == w_dev - 1, cf[1, t, hr, :], pltpu.roll(v, w_dev - 1, 0))
        x3[t, r, :, 0:ch] = left.astype(BF16)
        x3[t, r, :, ch:2 * ch] = v16
        x3[t, r, :, 2 * ch:3 * ch] = right.astype(BF16)

    cf[:, own_t, own] = pad_c[:, own_t, own].astype(F32)

    @pl.loop(1, t_dev + 1)
    def _(t):
        for r in range(1, h_dev + 1):
            build(t, r)

    def early_edges():
        for s in hr_own + hc_own:
            s[1]()
        for b in (low, high):
            cf[:, own_t, b] = pad_c[:, own_t, b].astype(F32)

        @pl.loop(1, t_dev + 1)
        def _(t):
            for r in (0, h_dev + 1):
                build(t, r)

        cw_copy.wait()

    def taps(acc, t, h0, frames):
        for a in frames:
            for b in range(3):
                acc = acc + jnp.dot(
                    x3[t + a, pl.ds(h0 + b, CH)].reshape(CH * w_dev, 3 * ch), cw[a, b],
                    preferred_element_type=F32)
        return acc

    def start_taps(t):
        @pl.loop(0, cpt)
        def _(j):
            acc = latents[t, pl.ds(j * CH, CH)].astype(F32).reshape(CH * w_dev, ch)
            acc_buf[t, j] = taps(acc, t, j * CH, [a for a in range(3) if 1 <= t + a <= t_dev])

    frame_of = {"t-": 0, "t+": t_dev + 1}

    def halo_in(side):
        f = frame_of[side]
        for r in range(h_dev):
            pad_n[f, r + 1] = norm(raw[0 if f == 0 else 1, r]).astype(BF16)
        for s in ph_h[side][0]:
            s[0]()
        ph_wt[side][1]()
        for s in ph_h[side][1]:
            s[0]()
        cf[:, f, own] = pad_c[:, f, own].astype(F32)
        for r in range(1, h_dev + 1):
            build(f, r)

    def halo_end(side):
        f = frame_of[side]
        for s in ph_h[side][0] + ph_h[side][1]:
            s[1]()
        for b in (low, high):
            cf[:, f, b] = pad_c[:, f, b].astype(F32)
        for r in (0, h_dev + 1):
            build(f, r)

    def blk_copy(t):
        return pltpu.make_async_copy(out_block.at[t], blk_hbm.at[t], loc_sem.at[4 + t_dev + t])

    def finish(t):
        for j in range(cpt):
            h0 = j * CH
            blk = taps(acc_buf[t, j], t, h0, [a for a in range(3) if not 1 <= t + a <= t_dev])
            blk = blk.astype(BF16)
            out_block[t, pl.ds(h0, CH)] = blk.reshape(CH, w_dev, ch)
            blk = blk.astype(F32)
            for k in range(ch // 128):
                fbuf[k] = blk[:, k * 128:(k + 1) * 128]
            for k in range(ch // 128):
                for dw in range(2):
                    part = fbuf[k, pl.ds(dw, CH * cols_dev, stride=2), :].astype(BF16)
                    part = part.reshape(prow, 2, cols_dev, 128)
                    for dh in range(2):
                        lo = (dh * 2 + dw) * ch + k * 128
                        pat[iw, t, pl.ds(j * prow, prow), :, lo:lo + 128] = part[:, dh]
            if t == 0:
                send_own(0, j)
        blk_copy(t).start()

    def piece(src, t, i0):
        return pat.at[src, t, pl.ds(i0, prow)]

    sides = (("w+", 0), ("w-", 1))

    def send_own(t, only=None):
        for j in range(cpt) if only is None else (only,):
            c = t * cpt + j
            p = piece(iw, t, j * prow)
            for side, i in sides:
                @pl.when(has[side])
                def _():
                    rcopy(p, p, ag_s.at[i, 0, c], ag_r.at[i, 0, c], dev[side]).start()

    def relay(t, d):
        for j in range(cpt):
            c = t * cpt + j
            for side, i in sides:
                src = iw - d if i == 0 else iw + d
                here = src >= 0 if i == 0 else src < n_w
                p = piece(src, t, j * prow)

                @pl.when(here)
                def _():
                    rcopy(p, p, ag_s.at[i, d - 1, c], ag_r.at[i, d - 1, c], dev[side]).wait_recv()
                    if d < n_w - 1:
                        @pl.when(has[side])
                        def _():
                            rcopy(p, p, ag_s.at[i, d, c], ag_r.at[i, d, c], dev[side]).start()

    pair = n_h % 2 == 0
    part_rows = pd // 2 if pair else pd
    mine = pl.ds((ih % 2) * part_rows, part_rows) if pair else pl.ds(0, pd)
    other = {"ha": ih + 1 - 2 * (ih % 2)}
    theirs = pl.ds((1 - ih % 2) * part_rows, part_rows) if pair else None

    def w_copy(d, src):
        return rcopy(w_hbm.at[:, mine], wg.at[src, :, mine], w_s.at[d], w_r.at[d],
                     {"ta": lax.rem(it + d, n_t)})

    def w_hand(d, part):
        src = lax.rem(it + n_t - d, n_t)
        return rcopy(wg.at[src, :, part], wg.at[src, :, part], wf_s.at[d], wf_r.at[d], other)

    def w_start():
        for d in range(1, n_t):
            w_copy(d, it).start()

    def w_mid():
        for d in range(1, n_t):
            w_copy(d, lax.rem(it + n_t - d, n_t)).wait_recv()
            if pair:
                w_hand(d, mine).start()

    def w_end():
        own_w.wait()
        if pair:
            for d in range(1, n_t):
                w_hand(d, theirs).wait_recv()

    def head_at(step):
        return lax.rem(it + 1 + step, n_t)

    def rim(t, a):
        lo, hi, two = pl.ds(WIN, WIN), pl.ds(rows, WIN), pl.ds(2 * a, 2)
        return [halo_kv(t, 0, a, "h-", kv.at[t, lo, two], kv.at[t, pl.ds(rows + WIN, WIN), two]),
                halo_kv(t, 1, a, "h+", kv.at[t, hi, two], kv.at[t, pl.ds(0, WIN), two])]

    def halo_kv(t, i, a, side, src, dst):
        c = rcopy(src, dst, kv_s.at[t, i, a], kv_r.at[t, i, a], dev[side])
        return has[side], has[side[0] + opp[side[1]]], c

    def qkv(t, step):
        a = head_at(step)
        x = pat[:, t].reshape(n_w * rows * cols_dev, pd)
        w = jnp.concatenate([wg[a, s] for s in range(3)], axis=1)
        y = jnp.dot(x, w, preferred_element_type=F32).astype(BF16)
        y = y.reshape(n_w, rows, cols_dev, 3 * hd)
        for s in range(n_w):
            cc = pl.ds(s * cols_dev, cols_dev)
            q_buf[t, a, :, cc, :] = y[s, :, :, 0:hd]
            kv[t, pl.ds(WIN, rows), 2 * a, cc, :] = y[s, :, :, hd:2 * hd]
            kv[t, pl.ds(WIN, rows), 2 * a + 1, cc, :] = y[s, :, :, 2 * hd:3 * hd]
        for out, _, c in rim(t, a):
            @pl.when(out)
            def _():
                c.start()

    scale = hd ** (-0.5) * 1.4426950408889634

    def attend(t, step):
        a = head_at(step)
        for _, inn, c in rim(t, a):
            @pl.when(inn)
            def _():
                c.wait_recv()
        for b in range(rows // WIN):
            r = pl.ds(b * WIN, WIN)
            kr_ = pl.ds(b * WIN, 3 * WIN)
            q = q_buf[t, a, r].reshape(WIN * pc, hd)
            k = kv[t, kr_, 2 * a].reshape(3 * WIN * pc, hd)
            v = kv[t, kr_, 2 * a + 1].reshape(3 * WIN * pc, hd)
            s = lax.dot_general(q, k, (((1,), (1,)), ((), ())), preferred_element_type=F32)
            s = s + bias[b]
            m = jnp.max(s, axis=1, keepdims=True)
            e = jnp.exp2((s - m) * scale)
            z = jnp.sum(e, axis=1, keepdims=True)
            o = jnp.dot(e.astype(BF16), v, preferred_element_type=F32) / z
            o_buf[t, a, r] = o.astype(BF16).reshape(WIN, pc, hd)
        dst = out_att.at[it * t_dev + t]

        @pl.when(a != it)
        def _():
            rcopy(o_buf.at[t, a], dst, at_s.at[t, a], at_r.at[t, it], {"ta": a}).start()

        @pl.when(a == it)
        def _():
            pltpu.make_async_copy(o_buf.at[t, a], dst, loc_sem.at[2 + t]).start()

    ph_t["t-"][1]()
    ph_t["t+"][0]()
    w_start()

    halo_in("t-")
    if t_dev == 1:
        ph_t["t+"][1]()
        halo_in("t+")
    early_edges()
    start_taps(0)
    halo_end("t-")
    if t_dev == 1:
        halo_end("t+")
    finish(0)
    for t in range(1, t_dev):
        if t == t_dev - 1:
            ph_t["t+"][1]()
            halo_in("t+")
        start_taps(t)
        if t == t_dev - 1:
            halo_end("t+")
        finish(t)

    total_rows = rows * n_h
    bs = (WIN * pc, 3 * WIN * pc)
    qr = lax.broadcasted_iota(jnp.int32, bs, 0) // pc
    kr = lax.broadcasted_iota(jnp.int32, bs, 1) // pc - WIN
    for b in range(rows // WIN):
        kg = ih * rows + b * WIN + kr
        ok = (jnp.abs(qr - kr) <= WIN) & (kg >= 0) & (kg < total_rows)
        bias[b] = jnp.where(ok, 0.0, -1e30).astype(F32)

    for d in range(1, n_w - 1):
        relay(0, d)
    if t_dev > 1:
        send_own(1)
    w_mid()
    if n_w > 1:
        relay(0, n_w - 1)
    w_end()
    for t in range(t_dev):
        more = t + 1 < t_dev
        if more:
            @pl.loop(0, n_t)
            def _(step):
                qkv(t, step)
            steps = max(n_w - 2, 1)
            for d in range(1, steps + 1):
                if d < n_w - 1:
                    relay(t + 1, d)

                @pl.loop(n_t * (d - 1) // steps, n_t * d // steps)
                def _(step):
                    attend(t, step)
        else:
            qkv(t, 0)

            @pl.loop(0, n_t - 1)
            def _(step):
                qkv(t, step + 1)
                attend(t, step)
            attend(t, n_t - 1)
        if more:
            if t + 2 < t_dev:
                send_own(t + 2)
            if n_w > 1:
                relay(t + 1, n_w - 1)

    for t in range(t_dev):
        blk_copy(t).wait()
        pltpu.make_async_copy(o_buf.at[t, it], out_att.at[it * t_dev + t], loc_sem.at[2 + t]).wait()
        for d in range(1, n_t):
            src = lax.rem(it + d, n_t)
            rcopy(o_buf.at[t, src], out_att.at[src * t_dev + t], at_s.at[t, src], at_r.at[t, src],
                  {"ta": src}).wait()
        for a in range(n_t):
            for out, _, c in rim(t, a):
                @pl.when(out)
                def _():
                    c.wait_send()
    for s in (ph_w + list(ph_t.values()) + list(ph_wt.values()) + hr_own + hc_own
              + ph_h["t-"][0] + ph_h["t-"][1] + ph_h["t+"][0] + ph_h["t+"][1]):
        s[2]()
    for d in range(1, n_t):
        w_copy(d, it).wait_send()
        if pair:
            w_hand(d, mine).wait_send()
    for t in range(t_dev):
        for j in range(cpt):
            c = t * cpt + j
            for side, i in sides:
                for d in range(n_w - 1):
                    src = iw - d if i == 0 else iw + d
                    here = src >= 0 if i == 0 else src < n_w
                    p = piece(src, t, j * prow)

                    @pl.when(here & has[side])
                    def _():
                        rcopy(p, p, ag_s.at[i, d, c], ag_r.at[i, d, c], dev[side]).wait_send()


def results(block, att, out_block, out_att, sem):
    copies = [pltpu.make_async_copy(block.at[i], out_block.at[i], sem.at[i])
              for i in range(block.shape[0])]
    copies += [pltpu.make_async_copy(att.at[i], out_att.at[i], sem.at[block.shape[0] + i])
               for i in range(att.shape[0])]
    for c in copies:
        c.start()
    for c in copies:
        c.wait()


def local(latents, norm_gain, conv_weight, qkv_weight):
    n_t, n_h, n_w = (lax.axis_size(a) for a in ("ta", "ha", "wa"))
    t_dev, h_dev, w_dev, ch = latents.shape
    rows, cols_dev = h_dev // 2, w_dev // 2
    pd, head_dev, qkv_count, hd = qkv_weight.shape
    pc = n_w * cols_dev
    cw = conv_weight.reshape(3, 3, 3 * ch, ch)
    w2 = qkv_weight.transpose(1, 2, 0, 3).reshape(qkv_count, pd, hd)
    frames = n_t * t_dev
    chunks = t_dev * (h_dev // CH)
    hbm = pl.BlockSpec(memory_space=pltpu.HBM)
    dma = pltpu.SemaphoreType.DMA
    block_out, att = pl.pallas_call(
        functools.partial(kernel, n_t, n_h, n_w),
        out_shape=(jax.ShapeDtypeStruct(latents.shape, BF16),
                   jax.ShapeDtypeStruct((frames, rows, pc, hd), BF16)),
        in_specs=[hbm, hbm, hbm, hbm],
        out_specs=(hbm, hbm),
        scratch_shapes=[
            pltpu.VMEM(latents.shape, BF16),
            pltpu.VMEM(latents.shape, BF16),
            pltpu.VMEM((1, ch), F32),
            pltpu.VMEM((2, h_dev, w_dev, ch), BF16),
            pltpu.VMEM((t_dev + 2, h_dev + 2, w_dev, ch), BF16),
            pltpu.VMEM((2, t_dev, h_dev, ch), F32),
            pltpu.VMEM((2, t_dev, h_dev, ch), BF16),
            pltpu.VMEM((2, t_dev + 2, 3 * h_dev, ch), BF16),
            pltpu.VMEM((2, t_dev + 2, 3 * h_dev, ch), F32),
            pltpu.VMEM((t_dev + 2, h_dev + 2, w_dev, 3 * ch), BF16),
            pltpu.VMEM((t_dev, h_dev // CH, CH * w_dev, ch), F32),
            pltpu.VMEM((3, 3, 3 * ch, ch), BF16),
            pltpu.VMEM((n_t, qkv_count, pd, hd), BF16),
            pltpu.VMEM((ch // 128, CH * w_dev, 128), F32),
            pltpu.VMEM((n_w, t_dev, rows, cols_dev, pd), BF16),
            pltpu.VMEM((t_dev, n_t, rows, pc, hd), BF16),
            pltpu.VMEM((t_dev, rows + 2 * WIN, 2 * n_t, pc, hd), BF16),
            pltpu.VMEM((rows // WIN, WIN * pc, 3 * WIN * pc), F32),
            pltpu.VMEM((t_dev, n_t, rows, pc, hd), BF16),
            dma((4 + 2 * t_dev,)),
            dma((18,)), dma((18,)),
            dma((n_t,)), dma((n_t,)),
            dma((n_t,)), dma((n_t,)),
            dma((2, n_w, chunks)), dma((2, n_w, chunks)),
            dma((t_dev, 2, n_t)), dma((t_dev, 2, n_t)),
            dma((t_dev, n_t)), dma((t_dev, n_t)),
        ],
        compiler_params=pltpu.CompilerParams(
            collective_id=0, has_side_effects=True, vmem_limit_bytes=58 * 1024 * 1024),
    )(latents, norm_gain.reshape(1, ch), cw, w2)
    block_out, att = pl.pallas_call(
        results,
        out_shape=(jax.ShapeDtypeStruct(block_out.shape, BF16), jax.ShapeDtypeStruct(att.shape, BF16)),
        in_specs=[hbm, hbm],
        out_specs=(hbm, hbm),
        scratch_shapes=[dma((t_dev + frames,))],
    )(block_out, att)
    return block_out, att.reshape(frames, rows, pc, head_dev, hd)


def solution(mesh):
    return jax.shard_map(
        local,
        mesh=mesh,
        in_specs=(P("ta", "ha", "wa", None), P(), P(), P(None, ("ta", "wa"), None, None)),
        out_specs=(P("ta", "ha", "wa", None), P(None, "ha", None, ("ta", "wa"), None)),
        check_vma=False,
    )
```

```python
import functools

import jax
import jax.numpy as jnp
from jax import lax
from jax.experimental import pallas as pl
from jax.experimental.pallas import tpu as pltpu
from jax.sharding import PartitionSpec as P

WIN = 4
STRIP = 32
CH = 8
MESH = pl.DeviceIdType.MESH
F32 = jnp.float32
BF16 = jnp.bfloat16


def kernel(n_t, n_h, n_w, lat_hbm, gain_hbm, cw_hbm, w_hbm, blk_hbm, out_att,
           out_block, latents, gain, raw, pad_n, edge_f, edge_b, pad_c, cf, x3, acc_buf, cw, wg, fbuf, pat, q_buf, kv, bias, s_buf, p_buf, o_buf,
           loc_sem, halo_s, halo_r, w_s, w_r, wf_s, wf_r, ag_s, ag_r, kv_s, kv_r, at_s, at_r):
    t_dev, h_dev, w_dev, ch = latents.shape
    rows = h_dev // 2
    cols_dev = w_dev // 2
    hd = q_buf.shape[-1]
    pd = pat.shape[-1]
    pc = n_w * cols_dev
    cpt = h_dev // CH
    prow = CH // 2
    it, ih, iw = lax.axis_index("ta"), lax.axis_index("ha"), lax.axis_index("wa")
    has = {"t-": it > 0, "t+": it < n_t - 1, "h-": ih > 0, "h+": ih < n_h - 1,
           "w-": iw > 0, "w+": iw < n_w - 1}
    opp = {"-": "+", "+": "-"}
    dev = {"t-": {"ta": it - 1}, "t+": {"ta": it + 1}, "h-": {"ha": ih - 1}, "h+": {"ha": ih + 1},
           "w-": {"wa": iw - 1}, "w+": {"wa": iw + 1}}

    def rcopy(src, dst, ss, rs, device):
        return pltpu.make_async_remote_copy(
            src_ref=src, dst_ref=dst, send_sem=ss, recv_sem=rs, device_id=device, device_id_type=MESH)

    lat_copy = pltpu.make_async_copy(lat_hbm, latents, loc_sem.at[2 + t_dev])
    lat_copy.start()
    gain_copy = pltpu.make_async_copy(gain_hbm, gain, loc_sem.at[3 + t_dev])
    gain_copy.start()
    cw_copy = pltpu.make_async_copy(cw_hbm, cw, loc_sem.at[0])
    cw_copy.start()
    own_w = pltpu.make_async_copy(w_hbm, wg.at[it], loc_sem.at[1])
    own_w.start()

    bar = pltpu.get_barrier_semaphore()
    count = jnp.int32(n_t - 1)
    for side in ("h-", "h+", "w-", "w+"):
        count = count + has[side].astype(jnp.int32)

        @pl.when(has[side])
        def _():
            pl.semaphore_signal(bar, inc=1, device_id=dev[side], device_id_type=MESH)
    for d in range(1, n_t):
        pl.semaphore_signal(bar, inc=1, device_id={"ta": lax.rem(it + d, n_t)}, device_id_type=MESH)

    pl.semaphore_wait(bar, count)

    def halo(i, side, src, dst):
        c = rcopy(src, dst, halo_s.at[i], halo_r.at[i], dev[side])
        from_side = side[0] + opp[side[1]]

        def start():
            @pl.when(has[side])
            def _():
                c.start()

        def recv():
            @pl.when(has[from_side])
            def _():
                c.wait_recv()

        def sent():
            @pl.when(has[side])
            def _():
                c.wait_send()
        return start, recv, sent

    own = pl.ds(h_dev, h_dev)
    low = pl.ds(0, h_dev)
    high = pl.ds(2 * h_dev, h_dev)
    own_t = pl.ds(1, t_dev)
    own_h = pl.ds(1, h_dev)
    ph_w = [halo(0, "w-", edge_b.at[0], pad_c.at[1, own_t, own]),
            halo(1, "w+", edge_b.at[1], pad_c.at[0, own_t, own])]
    ph_t = {"t+": halo(2, "t-", lat_hbm.at[0], raw.at[1]),
            "t-": halo(3, "t+", lat_hbm.at[t_dev - 1], raw.at[0])}
    ph_wt = {"t+": halo(4, "t-", pad_c.at[:, 1, own], pad_c.at[:, t_dev + 1, own]),
             "t-": halo(5, "t+", pad_c.at[:, t_dev, own], pad_c.at[:, 0, own])}

    def rows_cols(i, ts):
        return ([halo(i, "h-", pad_n.at[ts, 1], pad_n.at[ts, h_dev + 1]),
                 halo(i + 1, "h+", pad_n.at[ts, h_dev], pad_n.at[ts, 0])],
                [halo(i + 2, "h-", pad_c.at[:, ts, own], pad_c.at[:, ts, high]),
                 halo(i + 3, "h+", pad_c.at[:, ts, own], pad_c.at[:, ts, low])])

    hr_own, hc_own = rows_cols(6, own_t)
    ph_h = {"t-": rows_cols(10, pl.ds(0, 1)), "t+": rows_cols(14, pl.ds(t_dev + 1, 1))}
    ph_t["t-"][0]()

    def norm(x16):
        x = x16.astype(F32)
        ms = jnp.sum(x * x, axis=-1, keepdims=True) * (1.0 / ch)
        n = x * lax.rsqrt(ms + 1e-06) * half_gain
        return n * jnp.tanh(n) + n

    lat_copy.wait()
    gain_copy.wait()
    half_gain = gain[...] * 0.5

    @pl.loop(0, t_dev)
    def _(t):
        for r in range(h_dev):
            n = norm(latents[t, r])
            pad_n[t + 1, r + 1] = n.astype(BF16)
            edge_f[0, t, r:r + 1, :] = n[0:1]
            edge_f[1, t, r:r + 1, :] = n[w_dev - 1:w_dev]

    edge_b[...] = edge_f[...].astype(BF16)
    for s in ph_w + hr_own:
        s[0]()

    def zero(cond, ref, idx, shape):
        @pl.when(cond)
        def _():
            ref[idx] = jnp.zeros(shape, ref.dtype)

    no = {k: jnp.logical_not(v) for k, v in has.items()}
    full = slice(None)
    for side, s in (("w-", 0), ("w+", 1)):
        zero(no[side], pad_c, (s, own_t, own), (t_dev, h_dev, ch))
    for side, t in (("t-", 0), ("t+", t_dev + 1)):
        zero(no[side], pad_c, (full, t, own), (2, h_dev, ch))
        zero(no[side], raw, (0 if t == 0 else 1,), (h_dev, w_dev, ch))
    for side, r, b in (("h-", 0, low), ("h+", h_dev + 1, high)):
        zero(no[side], pad_n, (full, r), (t_dev + 2, w_dev, ch))
        zero(no[side], pad_c, (full, full, b), (2, t_dev + 2, h_dev, ch))
        zero(no[side], kv, (full, pl.ds(0 if side == "h-" else rows + WIN, WIN)),
             (t_dev, WIN) + kv.shape[2:])

    for s in ph_w:
        s[1]()
    for s in list(ph_wt.values()) + hc_own:
        s[0]()

    edge = lax.broadcasted_iota(jnp.int32, (w_dev, ch), 0)

    def build(t, r):
        v16 = pad_n[t, r]
        v = v16.astype(F32)
        hr = pl.ds(h_dev - 1 + r, 1)
        left = jnp.where(edge == 0, cf[0, t, hr, :], pltpu.roll(v, 1, 0))
        right = jnp.where(edge == w_dev - 1, cf[1, t, hr, :], pltpu.roll(v, w_dev - 1, 0))
        x3[t, r, :, 0:ch] = left.astype(BF16)
        x3[t, r, :, ch:2 * ch] = v16
        x3[t, r, :, 2 * ch:3 * ch] = right.astype(BF16)

    cf[:, own_t, own] = pad_c[:, own_t, own].astype(F32)

    @pl.loop(1, t_dev + 1)
    def _(t):
        for r in range(1, h_dev + 1):
            build(t, r)

    def early_edges():
        for s in hr_own + hc_own:
            s[1]()
        for b in (low, high):
            cf[:, own_t, b] = pad_c[:, own_t, b].astype(F32)

        @pl.loop(1, t_dev + 1)
        def _(t):
            for r in (0, h_dev + 1):
                build(t, r)

        cw_copy.wait()

    def taps(acc, t, h0, frames):
        for a in frames:
            for b in range(3):
                acc = acc + jnp.dot(
                    x3[t + a, pl.ds(h0 + b, CH)].reshape(CH * w_dev, 3 * ch), cw[a, b],
                    preferred_element_type=F32)
        return acc

    def start_taps(t):
        @pl.loop(0, cpt)
        def _(j):
            acc = latents[t, pl.ds(j * CH, CH)].astype(F32).reshape(CH * w_dev, ch)
            acc_buf[t, j] = taps(acc, t, j * CH, [a for a in range(3) if 1 <= t + a <= t_dev])

    frame_of = {"t-": 0, "t+": t_dev + 1}

    def halo_in(side):
        f = frame_of[side]
        for r in range(h_dev):
            pad_n[f, r + 1] = norm(raw[0 if f == 0 else 1, r]).astype(BF16)
        for s in ph_h[side][0]:
            s[0]()
        ph_wt[side][1]()
        for s in ph_h[side][1]:
            s[0]()
        cf[:, f, own] = pad_c[:, f, own].astype(F32)
        for r in range(1, h_dev + 1):
            build(f, r)

    def halo_end(side):
        f = frame_of[side]
        for s in ph_h[side][0] + ph_h[side][1]:
            s[1]()
        for b in (low, high):
            cf[:, f, b] = pad_c[:, f, b].astype(F32)
        for r in (0, h_dev + 1):
            build(f, r)

    def blk_copy(t):
        return pltpu.make_async_copy(out_block.at[t], blk_hbm.at[t], loc_sem.at[4 + t_dev + t])

    def finish(t):
        for j in range(cpt):
            h0 = j * CH
            blk = taps(acc_buf[t, j], t, h0, [a for a in range(3) if not 1 <= t + a <= t_dev])
            blk = blk.astype(BF16)
            out_block[t, pl.ds(h0, CH)] = blk.reshape(CH, w_dev, ch)
            blk = blk.astype(F32)
            for k in range(ch // 128):
                fbuf[k] = blk[:, k * 128:(k + 1) * 128]
            for k in range(ch // 128):
                for dw in range(2):
                    part = fbuf[k, pl.ds(dw, CH * cols_dev, stride=2), :].astype(BF16)
                    part = part.reshape(prow, 2, cols_dev, 128)
                    for dh in range(2):
                        lo = (dh * 2 + dw) * ch + k * 128
                        pat[iw, t, pl.ds(j * prow, prow), :, lo:lo + 128] = part[:, dh]
            if t == 0:
                send_own(0, j)
        blk_copy(t).start()

    def piece(src, t, i0):
        return pat.at[src, t, pl.ds(i0, prow)]

    sides = (("w+", 0), ("w-", 1))

    def send_own(t, only=None):
        for j in range(cpt) if only is None else (only,):
            c = t * cpt + j
            p = piece(iw, t, j * prow)
            for side, i in sides:
                @pl.when(has[side])
                def _():
                    rcopy(p, p, ag_s.at[i, 0, c], ag_r.at[i, 0, c], dev[side]).start()

    def relay(t, d):
        for j in range(cpt):
            c = t * cpt + j
            for side, i in sides:
                src = iw - d if i == 0 else iw + d
                here = src >= 0 if i == 0 else src < n_w
                p = piece(src, t, j * prow)

                @pl.when(here)
                def _():
                    rcopy(p, p, ag_s.at[i, d - 1, c], ag_r.at[i, d - 1, c], dev[side]).wait_recv()
                    if d < n_w - 1:
                        @pl.when(has[side])
                        def _():
                            rcopy(p, p, ag_s.at[i, d, c], ag_r.at[i, d, c], dev[side]).start()

    pair = n_h % 2 == 0
    part_rows = pd // 2 if pair else pd
    mine = pl.ds((ih % 2) * part_rows, part_rows) if pair else pl.ds(0, pd)
    other = {"ha": ih + 1 - 2 * (ih % 2)}
    theirs = pl.ds((1 - ih % 2) * part_rows, part_rows) if pair else None

    def w_copy(d, src):
        return rcopy(w_hbm.at[:, mine], wg.at[src, :, mine], w_s.at[d], w_r.at[d],
                     {"ta": lax.rem(it + d, n_t)})

    def w_hand(d, part):
        src = lax.rem(it + n_t - d, n_t)
        return rcopy(wg.at[src, :, part], wg.at[src, :, part], wf_s.at[d], wf_r.at[d], other)

    def w_start():
        for d in range(1, n_t):
            w_copy(d, it).start()

    def w_mid():
        for d in range(1, n_t):
            w_copy(d, lax.rem(it + n_t - d, n_t)).wait_recv()
            if pair:
                w_hand(d, mine).start()

    def w_end():
        own_w.wait()
        if pair:
            for d in range(1, n_t):
                w_hand(d, theirs).wait_recv()

    def head_at(step):
        return lax.rem(it + 1 + step, n_t)

    def rim(t, a):
        lo, hi, two = pl.ds(WIN, WIN), pl.ds(rows, WIN), pl.ds(2 * a, 2)
        return [halo_kv(t, 0, a, "h-", kv.at[t, lo, two], kv.at[t, pl.ds(rows + WIN, WIN), two]),
                halo_kv(t, 1, a, "h+", kv.at[t, hi, two], kv.at[t, pl.ds(0, WIN), two])]

    def halo_kv(t, i, a, side, src, dst):
        c = rcopy(src, dst, kv_s.at[t, i, a], kv_r.at[t, i, a], dev[side])
        return has[side], has[side[0] + opp[side[1]]], c

    def qkv(t, step):
        a = head_at(step)
        x = pat[:, t].reshape(n_w * rows * cols_dev, pd)
        w = jnp.concatenate([wg[a, s] for s in range(3)], axis=1)
        y = jnp.dot(x, w, preferred_element_type=F32).astype(BF16)
        y = y.reshape(n_w, rows, cols_dev, 3 * hd)
        for s in range(n_w):
            cc = pl.ds(s * cols_dev, cols_dev)
            q_buf[t, a, :, cc, :] = y[s, :, :, 0:hd]
            kv[t, pl.ds(WIN, rows), 2 * a, cc, :] = y[s, :, :, hd:2 * hd]
            kv[t, pl.ds(WIN, rows), 2 * a + 1, cc, :] = y[s, :, :, 2 * hd:3 * hd]
        for out, _, c in rim(t, a):
            @pl.when(out)
            def _():
                c.start()

    scale = hd ** (-0.5) * 1.4426950408889634

    def window(i):
        lo = i // pc * pc // 128 * 128
        hi = min(-(-(((i + STRIP - 1) // pc + 2 * WIN + 1) * pc) // 128) * 128, 3 * WIN * pc)
        return pl.ds(lo, hi - lo)

    def attend(t, step):
        a = head_at(step)
        for _, inn, c in rim(t, a):
            @pl.when(inn)
            def _():
                c.wait_recv()
        for b in range(rows // WIN):
            r = pl.ds(b * WIN, WIN)
            kr_ = pl.ds(b * WIN, 3 * WIN)
            q = q_buf[t, a, r].reshape(WIN * pc, hd)
            k = kv[t, kr_, 2 * a].reshape(3 * WIN * pc, hd)
            v = kv[t, kr_, 2 * a + 1].reshape(3 * WIN * pc, hd)
            s_buf[b] = lax.dot_general(q, k, (((1,), (1,)), ((), ())), preferred_element_type=F32)
            inv = []
            for i in range(0, WIN * pc, STRIP):
                at = (b, pl.ds(i, STRIP), window(i))
                s = s_buf[at] + bias[at]
                m = jnp.max(s, axis=1, keepdims=True)
                e = jnp.exp2((s - m) * scale)
                inv.append(1.0 / jnp.sum(e, axis=1, keepdims=True))
                p_buf[at] = e.astype(BF16)
            o = jnp.dot(p_buf[b], v, preferred_element_type=F32)
            o = o * jnp.concatenate(inv, axis=0)
            o_buf[t, a, r] = o.astype(BF16).reshape(WIN, pc, hd)
        dst = out_att.at[it * t_dev + t]

        @pl.when(a != it)
        def _():
            rcopy(o_buf.at[t, a], dst, at_s.at[t, a], at_r.at[t, it], {"ta": a}).start()

        @pl.when(a == it)
        def _():
            pltpu.make_async_copy(o_buf.at[t, a], dst, loc_sem.at[2 + t]).start()

    ph_t["t-"][1]()
    ph_t["t+"][0]()
    w_start()

    halo_in("t-")
    if t_dev == 1:
        ph_t["t+"][1]()
        halo_in("t+")
    early_edges()
    start_taps(0)
    halo_end("t-")
    if t_dev == 1:
        halo_end("t+")
    finish(0)
    for t in range(1, t_dev):
        if t == t_dev - 1:
            ph_t["t+"][1]()
            halo_in("t+")
        start_taps(t)
        if t == t_dev - 1:
            halo_end("t+")
        finish(t)

    total_rows = rows * n_h
    bs = (WIN * pc, 3 * WIN * pc)
    qr = lax.broadcasted_iota(jnp.int32, bs, 0) // pc
    kr = lax.broadcasted_iota(jnp.int32, bs, 1) // pc - WIN
    for b in range(rows // WIN):
        kg = ih * rows + b * WIN + kr
        ok = (jnp.abs(qr - kr) <= WIN) & (kg >= 0) & (kg < total_rows)
        bias[b] = jnp.where(ok, 0.0, -1e30).astype(F32)
        p_buf[b] = jnp.zeros(bs, BF16)

    for d in range(1, n_w - 1):
        relay(0, d)
    if t_dev > 1:
        send_own(1)
    w_mid()
    if n_w > 1:
        relay(0, n_w - 1)
    w_end()
    for t in range(t_dev):
        more = t + 1 < t_dev
        if more:
            @pl.loop(0, n_t)
            def _(step):
                qkv(t, step)
            steps = max(n_w - 2, 1)
            for d in range(1, steps + 1):
                if d < n_w - 1:
                    relay(t + 1, d)

                @pl.loop(n_t * (d - 1) // steps, n_t * d // steps)
                def _(step):
                    attend(t, step)
        else:
            qkv(t, 0)

            @pl.loop(0, n_t - 1)
            def _(step):
                qkv(t, step + 1)
                attend(t, step)
            attend(t, n_t - 1)
        if more:
            if t + 2 < t_dev:
                send_own(t + 2)
            if n_w > 1:
                relay(t + 1, n_w - 1)

    for t in range(t_dev):
        blk_copy(t).wait()
        pltpu.make_async_copy(o_buf.at[t, it], out_att.at[it * t_dev + t], loc_sem.at[2 + t]).wait()
        for d in range(1, n_t):
            src = lax.rem(it + d, n_t)
            rcopy(o_buf.at[t, src], out_att.at[src * t_dev + t], at_s.at[t, src], at_r.at[t, src],
                  {"ta": src}).wait()
        for a in range(n_t):
            for out, _, c in rim(t, a):
                @pl.when(out)
                def _():
                    c.wait_send()
    for s in (ph_w + list(ph_t.values()) + list(ph_wt.values()) + hr_own + hc_own
              + ph_h["t-"][0] + ph_h["t-"][1] + ph_h["t+"][0] + ph_h["t+"][1]):
        s[2]()
    for d in range(1, n_t):
        w_copy(d, it).wait_send()
        if pair:
            w_hand(d, mine).wait_send()
    for t in range(t_dev):
        for j in range(cpt):
            c = t * cpt + j
            for side, i in sides:
                for d in range(n_w - 1):
                    src = iw - d if i == 0 else iw + d
                    here = src >= 0 if i == 0 else src < n_w
                    p = piece(src, t, j * prow)

                    @pl.when(here & has[side])
                    def _():
                        rcopy(p, p, ag_s.at[i, d, c], ag_r.at[i, d, c], dev[side]).wait_send()


def results(block, att, out_block, out_att, sem):
    copies = [pltpu.make_async_copy(block, out_block, sem.at[0]),
              pltpu.make_async_copy(att, out_att, sem.at[1])]
    for c in copies:
        c.start()
    for c in copies:
        c.wait()


def local(latents, norm_gain, conv_weight, qkv_weight):
    n_t, n_h, n_w = (lax.axis_size(a) for a in ("ta", "ha", "wa"))
    t_dev, h_dev, w_dev, ch = latents.shape
    rows, cols_dev = h_dev // 2, w_dev // 2
    pd, head_dev, qkv_count, hd = qkv_weight.shape
    pc = n_w * cols_dev
    cw = conv_weight.reshape(3, 3, 3 * ch, ch)
    w2 = qkv_weight.transpose(1, 2, 0, 3).reshape(qkv_count, pd, hd)
    frames = n_t * t_dev
    chunks = t_dev * (h_dev // CH)
    vm = pl.BlockSpec(memory_space=pltpu.VMEM)
    hbm = pl.BlockSpec(memory_space=pltpu.HBM)
    dma = pltpu.SemaphoreType.DMA
    block_out, att = pl.pallas_call(
        functools.partial(kernel, n_t, n_h, n_w),
        out_shape=(jax.ShapeDtypeStruct(latents.shape, BF16),
                   jax.ShapeDtypeStruct((frames, rows, pc, hd), BF16)),
        in_specs=[hbm, hbm, hbm, hbm],
        out_specs=(hbm, hbm),
        scratch_shapes=[
            pltpu.VMEM(latents.shape, BF16),
            pltpu.VMEM(latents.shape, BF16),
            pltpu.VMEM((1, ch), F32),
            pltpu.VMEM((2, h_dev, w_dev, ch), BF16),
            pltpu.VMEM((t_dev + 2, h_dev + 2, w_dev, ch), BF16),
            pltpu.VMEM((2, t_dev, h_dev, ch), F32),
            pltpu.VMEM((2, t_dev, h_dev, ch), BF16),
            pltpu.VMEM((2, t_dev + 2, 3 * h_dev, ch), BF16),
            pltpu.VMEM((2, t_dev + 2, 3 * h_dev, ch), F32),
            pltpu.VMEM((t_dev + 2, h_dev + 2, w_dev, 3 * ch), BF16),
            pltpu.VMEM((t_dev, h_dev // CH, CH * w_dev, ch), F32),
            pltpu.VMEM((3, 3, 3 * ch, ch), BF16),
            pltpu.VMEM((n_t, qkv_count, pd, hd), BF16),
            pltpu.VMEM((ch // 128, CH * w_dev, 128), F32),
            pltpu.VMEM((n_w, t_dev, rows, cols_dev, pd), BF16),
            pltpu.VMEM((t_dev, n_t, rows, pc, hd), BF16),
            pltpu.VMEM((t_dev, rows + 2 * WIN, 2 * n_t, pc, hd), BF16),
            pltpu.VMEM((rows // WIN, WIN * pc, 3 * WIN * pc), F32),
            pltpu.VMEM((rows // WIN, WIN * pc, 3 * WIN * pc), F32),
            pltpu.VMEM((rows // WIN, WIN * pc, 3 * WIN * pc), BF16),
            pltpu.VMEM((t_dev, n_t, rows, pc, hd), BF16),
            dma((4 + 2 * t_dev,)),
            dma((18,)), dma((18,)),
            dma((n_t,)), dma((n_t,)),
            dma((n_t,)), dma((n_t,)),
            dma((2, n_w, chunks)), dma((2, n_w, chunks)),
            dma((t_dev, 2, n_t)), dma((t_dev, 2, n_t)),
            dma((t_dev, n_t)), dma((t_dev, n_t)),
        ],
        compiler_params=pltpu.CompilerParams(
            collective_id=0, has_side_effects=True, vmem_limit_bytes=58 * 1024 * 1024),
    )(latents, norm_gain.reshape(1, ch), cw, w2)
    block_out, att = pl.pallas_call(
        results,
        out_shape=(jax.ShapeDtypeStruct(block_out.shape, BF16), jax.ShapeDtypeStruct(att.shape, BF16)),
        in_specs=[vm, vm],
        out_specs=(hbm, hbm),
        scratch_shapes=[dma((2,))],
    )(block_out, att)
    return block_out, att.reshape(frames, rows, pc, head_dev, hd)


def solution(mesh):
    return jax.shard_map(
        local,
        mesh=mesh,
        in_specs=(P("ta", "ha", "wa", None), P(), P(), P(None, ("ta", "wa"), None, None)),
        out_specs=(P("ta", "ha", "wa", None), P(None, "ha", None, ("ta", "wa"), None)),
        check_vma=False,
    )
```

```python
import functools

import jax
import jax.numpy as jnp
from jax import lax
from jax.experimental import pallas as pl
from jax.experimental.pallas import tpu as pltpu
from jax.sharding import PartitionSpec as P

WIN = 4
STRIP = 32
CH = 8
MESH = pl.DeviceIdType.MESH
F32 = jnp.float32
BF16 = jnp.bfloat16


def kernel(n_t, n_h, n_w, lat_hbm, gain_hbm, cw_hbm, w_hbm, blk_hbm, out_att,
           out_block, latents, gain, raw, pad_n, edge_f, edge_b, pad_c, cf, x3, acc_buf, cw, wg, fbuf, pat, q_buf, kv, bias, s_buf, p_buf, o_buf,
           loc_sem, halo_s, halo_r, w_s, w_r, wf_s, wf_r, ag_s, ag_r, kv_s, kv_r, at_s, at_r):
    t_dev, h_dev, w_dev, ch = latents.shape
    rows = h_dev // 2
    cols_dev = w_dev // 2
    hd = q_buf.shape[-1]
    pd = pat.shape[-1]
    pc = n_w * cols_dev
    cpt = h_dev // CH
    prow = CH // 2
    it, ih, iw = lax.axis_index("ta"), lax.axis_index("ha"), lax.axis_index("wa")
    has = {"t-": it > 0, "t+": it < n_t - 1, "h-": ih > 0, "h+": ih < n_h - 1,
           "w-": iw > 0, "w+": iw < n_w - 1}
    opp = {"-": "+", "+": "-"}
    dev = {"t-": {"ta": it - 1}, "t+": {"ta": it + 1}, "h-": {"ha": ih - 1}, "h+": {"ha": ih + 1},
           "w-": {"wa": iw - 1}, "w+": {"wa": iw + 1}}

    def rcopy(src, dst, ss, rs, device):
        return pltpu.make_async_remote_copy(
            src_ref=src, dst_ref=dst, send_sem=ss, recv_sem=rs, device_id=device, device_id_type=MESH)

    lat_copy = pltpu.make_async_copy(lat_hbm, latents, loc_sem.at[2 + t_dev])
    lat_copy.start()
    gain_copy = pltpu.make_async_copy(gain_hbm, gain, loc_sem.at[3 + t_dev])
    gain_copy.start()
    cw_copy = pltpu.make_async_copy(cw_hbm, cw, loc_sem.at[0])
    cw_copy.start()
    own_w = pltpu.make_async_copy(w_hbm, wg.at[it], loc_sem.at[1])
    own_w.start()

    bar = pltpu.get_barrier_semaphore()
    count = jnp.int32(n_t - 1)
    for side in ("h-", "h+", "w-", "w+"):
        count = count + has[side].astype(jnp.int32)

        @pl.when(has[side])
        def _():
            pl.semaphore_signal(bar, inc=1, device_id=dev[side], device_id_type=MESH)
    for d in range(1, n_t):
        pl.semaphore_signal(bar, inc=1, device_id={"ta": lax.rem(it + d, n_t)}, device_id_type=MESH)

    pl.semaphore_wait(bar, count)

    def halo(i, side, src, dst):
        c = rcopy(src, dst, halo_s.at[i], halo_r.at[i], dev[side])
        from_side = side[0] + opp[side[1]]

        def start():
            @pl.when(has[side])
            def _():
                c.start()

        def recv():
            @pl.when(has[from_side])
            def _():
                c.wait_recv()

        def sent():
            @pl.when(has[side])
            def _():
                c.wait_send()
        return start, recv, sent

    own = pl.ds(h_dev, h_dev)
    low = pl.ds(0, h_dev)
    high = pl.ds(2 * h_dev, h_dev)
    own_t = pl.ds(1, t_dev)
    own_h = pl.ds(1, h_dev)
    ph_w = [halo(0, "w-", edge_b.at[0], pad_c.at[1, own_t, own]),
            halo(1, "w+", edge_b.at[1], pad_c.at[0, own_t, own])]
    ph_t = {"t+": halo(2, "t-", lat_hbm.at[0], raw.at[1]),
            "t-": halo(3, "t+", lat_hbm.at[t_dev - 1], raw.at[0])}
    ph_wt = {"t+": halo(4, "t-", pad_c.at[:, 1, own], pad_c.at[:, t_dev + 1, own]),
             "t-": halo(5, "t+", pad_c.at[:, t_dev, own], pad_c.at[:, 0, own])}

    def rows_cols(i, ts):
        return ([halo(i, "h-", pad_n.at[ts, 1], pad_n.at[ts, h_dev + 1]),
                 halo(i + 1, "h+", pad_n.at[ts, h_dev], pad_n.at[ts, 0])],
                [halo(i + 2, "h-", pad_c.at[:, ts, own], pad_c.at[:, ts, high]),
                 halo(i + 3, "h+", pad_c.at[:, ts, own], pad_c.at[:, ts, low])])

    hr_own, hc_own = rows_cols(6, own_t)
    ph_h = {"t-": rows_cols(10, pl.ds(0, 1)), "t+": rows_cols(14, pl.ds(t_dev + 1, 1))}
    ph_t["t-"][0]()

    def norm(x16):
        x = x16.astype(F32)
        ms = jnp.sum(x * x, axis=-1, keepdims=True) * (1.0 / ch)
        n = x * lax.rsqrt(ms + 1e-06) * half_gain
        return n * jnp.tanh(n) + n

    lat_copy.wait()
    gain_copy.wait()
    half_gain = gain[...] * 0.5

    @pl.loop(0, t_dev)
    def _(t):
        for r in range(h_dev):
            n = norm(latents[t, r])
            pad_n[t + 1, r + 1] = n.astype(BF16)
            edge_f[0, t, r:r + 1, :] = n[0:1]
            edge_f[1, t, r:r + 1, :] = n[w_dev - 1:w_dev]

    edge_b[...] = edge_f[...].astype(BF16)
    for s in ph_w + hr_own:
        s[0]()

    def zero(cond, ref, idx, shape):
        @pl.when(cond)
        def _():
            ref[idx] = jnp.zeros(shape, ref.dtype)

    no = {k: jnp.logical_not(v) for k, v in has.items()}
    full = slice(None)
    for side, s in (("w-", 0), ("w+", 1)):
        zero(no[side], pad_c, (s, own_t, own), (t_dev, h_dev, ch))
    for side, t in (("t-", 0), ("t+", t_dev + 1)):
        zero(no[side], pad_c, (full, t, own), (2, h_dev, ch))
        zero(no[side], raw, (0 if t == 0 else 1,), (h_dev, w_dev, ch))
    for side, r, b in (("h-", 0, low), ("h+", h_dev + 1, high)):
        zero(no[side], pad_n, (full, r), (t_dev + 2, w_dev, ch))
        zero(no[side], pad_c, (full, full, b), (2, t_dev + 2, h_dev, ch))
        zero(no[side], kv, (full, pl.ds(0 if side == "h-" else rows + WIN, WIN)),
             (t_dev, WIN) + kv.shape[2:])

    for s in ph_w:
        s[1]()
    for s in list(ph_wt.values()) + hc_own:
        s[0]()

    edge = lax.broadcasted_iota(jnp.int32, (w_dev, ch), 0)

    def build(t, r):
        v16 = pad_n[t, r]
        v = v16.astype(F32)
        hr = pl.ds(h_dev - 1 + r, 1)
        left = jnp.where(edge == 0, cf[0, t, hr, :], pltpu.roll(v, 1, 0))
        right = jnp.where(edge == w_dev - 1, cf[1, t, hr, :], pltpu.roll(v, w_dev - 1, 0))
        x3[t, r, :, 0:ch] = left.astype(BF16)
        x3[t, r, :, ch:2 * ch] = v16
        x3[t, r, :, 2 * ch:3 * ch] = right.astype(BF16)

    cf[:, own_t, own] = pad_c[:, own_t, own].astype(F32)

    @pl.loop(1, t_dev + 1)
    def _(t):
        for r in range(1, h_dev + 1):
            build(t, r)

    def early_edges():
        for s in hr_own + hc_own:
            s[1]()
        for b in (low, high):
            cf[:, own_t, b] = pad_c[:, own_t, b].astype(F32)

        @pl.loop(1, t_dev + 1)
        def _(t):
            for r in (0, h_dev + 1):
                build(t, r)

        cw_copy.wait()

    def taps(acc, t, h0, frames):
        for a in frames:
            for b in range(3):
                acc = acc + jnp.dot(
                    x3[t + a, pl.ds(h0 + b, CH)].reshape(CH * w_dev, 3 * ch), cw[a, b],
                    preferred_element_type=F32)
        return acc

    def start_taps(t):
        @pl.loop(0, cpt)
        def _(j):
            acc = latents[t, pl.ds(j * CH, CH)].astype(F32).reshape(CH * w_dev, ch)
            acc_buf[t, j] = taps(acc, t, j * CH, [a for a in range(3) if 1 <= t + a <= t_dev])

    frame_of = {"t-": 0, "t+": t_dev + 1}

    def halo_in(side):
        f = frame_of[side]
        for r in range(h_dev):
            pad_n[f, r + 1] = norm(raw[0 if f == 0 else 1, r]).astype(BF16)
        for s in ph_h[side][0]:
            s[0]()
        ph_wt[side][1]()
        for s in ph_h[side][1]:
            s[0]()
        cf[:, f, own] = pad_c[:, f, own].astype(F32)
        for r in range(1, h_dev + 1):
            build(f, r)

    def halo_end(side):
        f = frame_of[side]
        for s in ph_h[side][0] + ph_h[side][1]:
            s[1]()
        for b in (low, high):
            cf[:, f, b] = pad_c[:, f, b].astype(F32)
        for r in (0, h_dev + 1):
            build(f, r)

    def blk_copy(t):
        return pltpu.make_async_copy(out_block.at[t], blk_hbm.at[t], loc_sem.at[4 + t_dev + t])

    def finish(t):
        for j in range(cpt):
            h0 = j * CH
            blk = taps(acc_buf[t, j], t, h0, [a for a in range(3) if not 1 <= t + a <= t_dev])
            blk = blk.astype(BF16)
            out_block[t, pl.ds(h0, CH)] = blk.reshape(CH, w_dev, ch)
            blk = blk.astype(F32)
            for k in range(ch // 128):
                fbuf[k] = blk[:, k * 128:(k + 1) * 128]
            for k in range(ch // 128):
                for dw in range(2):
                    part = fbuf[k, pl.ds(dw, CH * cols_dev, stride=2), :].astype(BF16)
                    part = part.reshape(prow, 2, cols_dev, 128)
                    for dh in range(2):
                        lo = (dh * 2 + dw) * ch + k * 128
                        pat[iw, t, pl.ds(j * prow, prow), :, lo:lo + 128] = part[:, dh]
            send_own(t, j)
        blk_copy(t).start()

    def piece(src, t, i0):
        return pat.at[src, t, pl.ds(i0, prow)]

    sides = (("w+", 0), ("w-", 1))

    def send_own(t, only=None):
        for j in range(cpt) if only is None else (only,):
            c = t * cpt + j
            p = piece(iw, t, j * prow)
            for side, i in sides:
                @pl.when(has[side])
                def _():
                    rcopy(p, p, ag_s.at[i, 0, c], ag_r.at[i, 0, c], dev[side]).start()

    def relay(t, d):
        for j in range(cpt):
            c = t * cpt + j
            for side, i in sides:
                src = iw - d if i == 0 else iw + d
                here = src >= 0 if i == 0 else src < n_w
                p = piece(src, t, j * prow)

                @pl.when(here)
                def _():
                    rcopy(p, p, ag_s.at[i, d - 1, c], ag_r.at[i, d - 1, c], dev[side]).wait_recv()
                    if d < n_w - 1:
                        @pl.when(has[side])
                        def _():
                            rcopy(p, p, ag_s.at[i, d, c], ag_r.at[i, d, c], dev[side]).start()

    pair = n_h % 2 == 0
    part_rows = pd // 2 if pair else pd
    mine = pl.ds((ih % 2) * part_rows, part_rows) if pair else pl.ds(0, pd)
    other = {"ha": ih + 1 - 2 * (ih % 2)}
    theirs = pl.ds((1 - ih % 2) * part_rows, part_rows) if pair else None

    def w_copy(d, src):
        return rcopy(w_hbm.at[:, mine], wg.at[src, :, mine], w_s.at[d], w_r.at[d],
                     {"ta": lax.rem(it + d, n_t)})

    def w_hand(d, part):
        src = lax.rem(it + n_t - d, n_t)
        return rcopy(wg.at[src, :, part], wg.at[src, :, part], wf_s.at[d], wf_r.at[d], other)

    w_left = list(range(1, n_t))

    def w_next(count=1):
        for d in w_left[:count]:
            w_copy(d, it).start()
        del w_left[:count]

    def w_mid():
        for d in range(1, n_t):
            w_copy(d, lax.rem(it + n_t - d, n_t)).wait_recv()
            if pair:
                w_hand(d, mine).start()

    def w_end():
        own_w.wait()
        if pair:
            for d in range(1, n_t):
                w_hand(d, theirs).wait_recv()

    def head_at(step):
        return lax.rem(it + 1 + step, n_t)

    def rim(t, a):
        lo, hi, two = pl.ds(WIN, WIN), pl.ds(rows, WIN), pl.ds(2 * a, 2)
        return [halo_kv(t, 0, a, "h-", kv.at[t, lo, two], kv.at[t, pl.ds(rows + WIN, WIN), two]),
                halo_kv(t, 1, a, "h+", kv.at[t, hi, two], kv.at[t, pl.ds(0, WIN), two])]

    def halo_kv(t, i, a, side, src, dst):
        c = rcopy(src, dst, kv_s.at[t, i, a], kv_r.at[t, i, a], dev[side])
        return has[side], has[side[0] + opp[side[1]]], c

    def qkv(t, step):
        a = head_at(step)
        x = pat[:, t].reshape(n_w * rows * cols_dev, pd)
        w = jnp.concatenate([wg[a, s] for s in range(3)], axis=1)
        y = jnp.dot(x, w, preferred_element_type=F32).astype(BF16)
        y = y.reshape(n_w, rows, cols_dev, 3 * hd)
        for s in range(n_w):
            cc = pl.ds(s * cols_dev, cols_dev)
            q_buf[t, a, :, cc, :] = y[s, :, :, 0:hd]
            kv[t, pl.ds(WIN, rows), 2 * a, cc, :] = y[s, :, :, hd:2 * hd]
            kv[t, pl.ds(WIN, rows), 2 * a + 1, cc, :] = y[s, :, :, 2 * hd:3 * hd]
        for out, _, c in rim(t, a):
            @pl.when(out)
            def _():
                c.start()

    scale = hd ** (-0.5) * 1.4426950408889634

    def window(i):
        lo = i // pc * pc // 128 * 128
        hi = min(-(-(((i + STRIP - 1) // pc + 2 * WIN + 1) * pc) // 128) * 128, 3 * WIN * pc)
        return pl.ds(lo, hi - lo)

    def attend(t, step):
        a = head_at(step)
        for _, inn, c in rim(t, a):
            @pl.when(inn)
            def _():
                c.wait_recv()
        for b in range(rows // WIN):
            r = pl.ds(b * WIN, WIN)
            kr_ = pl.ds(b * WIN, 3 * WIN)
            q = q_buf[t, a, r].reshape(WIN * pc, hd)
            k = kv[t, kr_, 2 * a].reshape(3 * WIN * pc, hd)
            v = kv[t, kr_, 2 * a + 1].reshape(3 * WIN * pc, hd)
            s_buf[b] = lax.dot_general(q, k, (((1,), (1,)), ((), ())), preferred_element_type=F32)
            inv = []
            for i in range(0, WIN * pc, STRIP):
                at = (b, pl.ds(i, STRIP), window(i))
                s = s_buf[at] + bias[at]
                m = jnp.max(s, axis=1, keepdims=True)
                e = jnp.exp2((s - m) * scale)
                inv.append(1.0 / jnp.sum(e, axis=1, keepdims=True))
                p_buf[at] = e.astype(BF16)
            o = jnp.dot(p_buf[b], v, preferred_element_type=F32)
            o = o * jnp.concatenate(inv, axis=0)
            o_buf[t, a, r] = o.astype(BF16).reshape(WIN, pc, hd)
        dst = out_att.at[it * t_dev + t]

        @pl.when(a != it)
        def _():
            rcopy(o_buf.at[t, a], dst, at_s.at[t, a], at_r.at[t, it], {"ta": a}).start()

        @pl.when(a == it)
        def _():
            pltpu.make_async_copy(o_buf.at[t, a], dst, loc_sem.at[2 + t]).start()

    ph_t["t-"][1]()
    ph_t["t+"][0]()

    halo_in("t-")
    if t_dev == 1:
        ph_t["t+"][1]()
        halo_in("t+")
    early_edges()
    start_taps(0)
    halo_end("t-")
    if t_dev == 1:
        halo_end("t+")
    finish(0)
    w_next()
    for t in range(1, t_dev):
        if t == t_dev - 1:
            ph_t["t+"][1]()
            halo_in("t+")
        start_taps(t)
        if t == t_dev - 1:
            halo_end("t+")
        finish(t)
        w_next()

    total_rows = rows * n_h
    bs = (WIN * pc, 3 * WIN * pc)
    qr = lax.broadcasted_iota(jnp.int32, bs, 0) // pc
    kr = lax.broadcasted_iota(jnp.int32, bs, 1) // pc - WIN
    for b in range(rows // WIN):
        kg = ih * rows + b * WIN + kr
        ok = (jnp.abs(qr - kr) <= WIN) & (kg >= 0) & (kg < total_rows)
        bias[b] = jnp.where(ok, 0.0, -1e30).astype(F32)
        p_buf[b] = jnp.zeros(bs, BF16)

    for d in range(1, n_w - 1):
        for t in range(t_dev):
            relay(t, d)
        w_next()
    w_next(n_t)
    w_mid()
    if n_w > 1:
        relay(0, n_w - 1)
    w_end()
    for t in range(t_dev):
        if t + 1 < t_dev:
            @pl.loop(0, n_t)
            def _(step):
                qkv(t, step)

            @pl.loop(0, n_t)
            def _(step):
                attend(t, step)
            if n_w > 1:
                relay(t + 1, n_w - 1)
        else:
            qkv(t, 0)

            @pl.loop(0, n_t - 1)
            def _(step):
                qkv(t, step + 1)
                attend(t, step)
            attend(t, n_t - 1)

    for t in range(t_dev):
        blk_copy(t).wait()
        pltpu.make_async_copy(o_buf.at[t, it], out_att.at[it * t_dev + t], loc_sem.at[2 + t]).wait()
        for d in range(1, n_t):
            src = lax.rem(it + d, n_t)
            rcopy(o_buf.at[t, src], out_att.at[src * t_dev + t], at_s.at[t, src], at_r.at[t, src],
                  {"ta": src}).wait()
        for a in range(n_t):
            for out, _, c in rim(t, a):
                @pl.when(out)
                def _():
                    c.wait_send()
    for s in (ph_w + list(ph_t.values()) + list(ph_wt.values()) + hr_own + hc_own
              + ph_h["t-"][0] + ph_h["t-"][1] + ph_h["t+"][0] + ph_h["t+"][1]):
        s[2]()
    for d in range(1, n_t):
        w_copy(d, it).wait_send()
        if pair:
            w_hand(d, mine).wait_send()
    for t in range(t_dev):
        for j in range(cpt):
            c = t * cpt + j
            for side, i in sides:
                for d in range(n_w - 1):
                    src = iw - d if i == 0 else iw + d
                    here = src >= 0 if i == 0 else src < n_w
                    p = piece(src, t, j * prow)

                    @pl.when(here & has[side])
                    def _():
                        rcopy(p, p, ag_s.at[i, d, c], ag_r.at[i, d, c], dev[side]).wait_send()


def results(block, att, out_block, out_att, sem):
    copies = [pltpu.make_async_copy(block, out_block, sem.at[0]),
              pltpu.make_async_copy(att, out_att, sem.at[1])]
    for c in copies:
        c.start()
    for c in copies:
        c.wait()


def local(latents, norm_gain, conv_weight, qkv_weight):
    n_t, n_h, n_w = (lax.axis_size(a) for a in ("ta", "ha", "wa"))
    t_dev, h_dev, w_dev, ch = latents.shape
    rows, cols_dev = h_dev // 2, w_dev // 2
    pd, head_dev, qkv_count, hd = qkv_weight.shape
    pc = n_w * cols_dev
    cw = conv_weight.reshape(3, 3, 3 * ch, ch)
    w2 = qkv_weight.transpose(1, 2, 0, 3).reshape(qkv_count, pd, hd)
    frames = n_t * t_dev
    chunks = t_dev * (h_dev // CH)
    vm = pl.BlockSpec(memory_space=pltpu.VMEM)
    hbm = pl.BlockSpec(memory_space=pltpu.HBM)
    dma = pltpu.SemaphoreType.DMA
    block_out, att = pl.pallas_call(
        functools.partial(kernel, n_t, n_h, n_w),
        out_shape=(jax.ShapeDtypeStruct(latents.shape, BF16),
                   jax.ShapeDtypeStruct((frames, rows, pc, hd), BF16)),
        in_specs=[hbm, hbm, hbm, hbm],
        out_specs=(hbm, hbm),
        scratch_shapes=[
            pltpu.VMEM(latents.shape, BF16),
            pltpu.VMEM(latents.shape, BF16),
            pltpu.VMEM((1, ch), F32),
            pltpu.VMEM((2, h_dev, w_dev, ch), BF16),
            pltpu.VMEM((t_dev + 2, h_dev + 2, w_dev, ch), BF16),
            pltpu.VMEM((2, t_dev, h_dev, ch), F32),
            pltpu.VMEM((2, t_dev, h_dev, ch), BF16),
            pltpu.VMEM((2, t_dev + 2, 3 * h_dev, ch), BF16),
            pltpu.VMEM((2, t_dev + 2, 3 * h_dev, ch), F32),
            pltpu.VMEM((t_dev + 2, h_dev + 2, w_dev, 3 * ch), BF16),
            pltpu.VMEM((t_dev, h_dev // CH, CH * w_dev, ch), F32),
            pltpu.VMEM((3, 3, 3 * ch, ch), BF16),
            pltpu.VMEM((n_t, qkv_count, pd, hd), BF16),
            pltpu.VMEM((ch // 128, CH * w_dev, 128), F32),
            pltpu.VMEM((n_w, t_dev, rows, cols_dev, pd), BF16),
            pltpu.VMEM((t_dev, n_t, rows, pc, hd), BF16),
            pltpu.VMEM((t_dev, rows + 2 * WIN, 2 * n_t, pc, hd), BF16),
            pltpu.VMEM((rows // WIN, WIN * pc, 3 * WIN * pc), F32),
            pltpu.VMEM((rows // WIN, WIN * pc, 3 * WIN * pc), F32),
            pltpu.VMEM((rows // WIN, WIN * pc, 3 * WIN * pc), BF16),
            pltpu.VMEM((t_dev, n_t, rows, pc, hd), BF16),
            dma((4 + 2 * t_dev,)),
            dma((18,)), dma((18,)),
            dma((n_t,)), dma((n_t,)),
            dma((n_t,)), dma((n_t,)),
            dma((2, n_w, chunks)), dma((2, n_w, chunks)),
            dma((t_dev, 2, n_t)), dma((t_dev, 2, n_t)),
            dma((t_dev, n_t)), dma((t_dev, n_t)),
        ],
        compiler_params=pltpu.CompilerParams(
            collective_id=0, has_side_effects=True, vmem_limit_bytes=58 * 1024 * 1024),
    )(latents, norm_gain.reshape(1, ch), cw, w2)
    block_out, att = pl.pallas_call(
        results,
        out_shape=(jax.ShapeDtypeStruct(block_out.shape, BF16), jax.ShapeDtypeStruct(att.shape, BF16)),
        in_specs=[vm, vm],
        out_specs=(hbm, hbm),
        scratch_shapes=[dma((2,))],
    )(block_out, att)
    return block_out, att.reshape(frames, rows, pc, head_dev, hd)


def solution(mesh):
    return jax.shard_map(
        local,
        mesh=mesh,
        in_specs=(P("ta", "ha", "wa", None), P(), P(), P(None, ("ta", "wa"), None, None)),
        out_specs=(P("ta", "ha", "wa", None), P(None, "ha", None, ("ta", "wa"), None)),
        check_vma=False,
    )
```

```python
import functools

import jax
import jax.numpy as jnp
from jax import lax
from jax.experimental import pallas as pl
from jax.experimental.pallas import tpu as pltpu
from jax.sharding import PartitionSpec as P

WIN = 4
STRIP = 32
CH = 16
PH = 8
MESH = pl.DeviceIdType.MESH
F32 = jnp.float32
BF16 = jnp.bfloat16


def kernel(n_t, n_h, n_w, lat_hbm, gain_hbm, cw_hbm, w_hbm, blk_hbm, out_att,
           out_block, latents, gain, raw, pad_n, edge_f, edge_b, pad_c, cf, x3, acc_buf, cw, wg, fbuf, pat, q_buf, kv, bias, s_buf, p_buf, o_buf,
           loc_sem, halo_s, halo_r, w_s, w_r, wf_s, wf_r, ag_s, ag_r, kv_s, kv_r, at_s, at_r):
    t_dev, h_dev, w_dev, ch = latents.shape
    rows = h_dev // 2
    cols_dev = w_dev // 2
    hd = q_buf.shape[-1]
    pd = pat.shape[-1]
    pc = n_w * cols_dev
    cpt = h_dev // CH
    prow = CH // 2
    ppt = h_dev // PH
    srow = PH // 2
    it, ih, iw = lax.axis_index("ta"), lax.axis_index("ha"), lax.axis_index("wa")
    has = {"t-": it > 0, "t+": it < n_t - 1, "h-": ih > 0, "h+": ih < n_h - 1,
           "w-": iw > 0, "w+": iw < n_w - 1}
    opp = {"-": "+", "+": "-"}
    dev = {"t-": {"ta": it - 1}, "t+": {"ta": it + 1}, "h-": {"ha": ih - 1}, "h+": {"ha": ih + 1},
           "w-": {"wa": iw - 1}, "w+": {"wa": iw + 1}}

    def rcopy(src, dst, ss, rs, device):
        return pltpu.make_async_remote_copy(
            src_ref=src, dst_ref=dst, send_sem=ss, recv_sem=rs, device_id=device, device_id_type=MESH)

    lat_copy = pltpu.make_async_copy(lat_hbm, latents, loc_sem.at[2 + t_dev])
    lat_copy.start()
    gain_copy = pltpu.make_async_copy(gain_hbm, gain, loc_sem.at[3 + t_dev])
    gain_copy.start()
    cw_copy = pltpu.make_async_copy(cw_hbm, cw, loc_sem.at[0])
    cw_copy.start()
    own_w = pltpu.make_async_copy(w_hbm, wg.at[it], loc_sem.at[1])
    own_w.start()

    bar = pltpu.get_barrier_semaphore()
    count = jnp.int32(n_t - 1)
    for side in ("h-", "h+", "w-", "w+"):
        count = count + has[side].astype(jnp.int32)

        @pl.when(has[side])
        def _():
            pl.semaphore_signal(bar, inc=1, device_id=dev[side], device_id_type=MESH)
    for d in range(1, n_t):
        pl.semaphore_signal(bar, inc=1, device_id={"ta": lax.rem(it + d, n_t)}, device_id_type=MESH)

    pl.semaphore_wait(bar, count)

    def halo(i, side, src, dst):
        c = rcopy(src, dst, halo_s.at[i], halo_r.at[i], dev[side])
        from_side = side[0] + opp[side[1]]

        def start():
            @pl.when(has[side])
            def _():
                c.start()

        def recv():
            @pl.when(has[from_side])
            def _():
                c.wait_recv()

        def sent():
            @pl.when(has[side])
            def _():
                c.wait_send()
        return start, recv, sent

    own = pl.ds(h_dev, h_dev)
    low = pl.ds(0, h_dev)
    high = pl.ds(2 * h_dev, h_dev)
    own_t = pl.ds(1, t_dev)
    own_h = pl.ds(1, h_dev)
    ph_w = [halo(0, "w-", edge_b.at[0], pad_c.at[1, own_t, own]),
            halo(1, "w+", edge_b.at[1], pad_c.at[0, own_t, own])]
    ph_t = {"t+": halo(2, "t-", lat_hbm.at[0], raw.at[1]),
            "t-": halo(3, "t+", lat_hbm.at[t_dev - 1], raw.at[0])}
    ph_wt = {"t+": halo(4, "t-", pad_c.at[:, 1, own], pad_c.at[:, t_dev + 1, own]),
             "t-": halo(5, "t+", pad_c.at[:, t_dev, own], pad_c.at[:, 0, own])}

    def rows_cols(i, ts):
        return ([halo(i, "h-", pad_n.at[ts, 1], pad_n.at[ts, h_dev + 1]),
                 halo(i + 1, "h+", pad_n.at[ts, h_dev], pad_n.at[ts, 0])],
                [halo(i + 2, "h-", pad_c.at[:, ts, own], pad_c.at[:, ts, high]),
                 halo(i + 3, "h+", pad_c.at[:, ts, own], pad_c.at[:, ts, low])])

    hr_own, hc_own = rows_cols(6, own_t)
    ph_h = {"t-": rows_cols(10, pl.ds(0, 1)), "t+": rows_cols(14, pl.ds(t_dev + 1, 1))}
    ph_t["t-"][0]()

    def norm(x16):
        x = x16.astype(F32)
        ms = jnp.sum(x * x, axis=-1, keepdims=True) * (1.0 / ch)
        n = x * lax.rsqrt(ms + 1e-06) * half_gain
        return n * jnp.tanh(n) + n

    lat_copy.wait()
    gain_copy.wait()
    half_gain = gain[...] * 0.5

    @pl.loop(0, t_dev)
    def _(t):
        for r in range(h_dev):
            n = norm(latents[t, r])
            pad_n[t + 1, r + 1] = n.astype(BF16)
            edge_f[0, t, r:r + 1, :] = n[0:1]
            edge_f[1, t, r:r + 1, :] = n[w_dev - 1:w_dev]

    edge_b[...] = edge_f[...].astype(BF16)
    for s in ph_w + hr_own:
        s[0]()

    def zero(cond, ref, idx, shape):
        @pl.when(cond)
        def _():
            ref[idx] = jnp.zeros(shape, ref.dtype)

    no = {k: jnp.logical_not(v) for k, v in has.items()}
    full = slice(None)
    for side, s in (("w-", 0), ("w+", 1)):
        zero(no[side], pad_c, (s, own_t, own), (t_dev, h_dev, ch))
    for side, t in (("t-", 0), ("t+", t_dev + 1)):
        zero(no[side], pad_c, (full, t, own), (2, h_dev, ch))
        zero(no[side], raw, (0 if t == 0 else 1,), (h_dev, w_dev, ch))
    for side, r, b in (("h-", 0, low), ("h+", h_dev + 1, high)):
        zero(no[side], pad_n, (full, r), (t_dev + 2, w_dev, ch))
        zero(no[side], pad_c, (full, full, b), (2, t_dev + 2, h_dev, ch))
        zero(no[side], kv, (full, pl.ds(0 if side == "h-" else rows + WIN, WIN)),
             (t_dev, WIN) + kv.shape[2:])

    for s in ph_w:
        s[1]()
    for s in list(ph_wt.values()) + hc_own:
        s[0]()

    edge = lax.broadcasted_iota(jnp.int32, (w_dev, ch), 0)

    def build(t, r):
        v16 = pad_n[t, r]
        v = v16.astype(F32)
        hr = pl.ds(h_dev - 1 + r, 1)
        left = jnp.where(edge == 0, cf[0, t, hr, :], pltpu.roll(v, 1, 0))
        right = jnp.where(edge == w_dev - 1, cf[1, t, hr, :], pltpu.roll(v, w_dev - 1, 0))
        x3[t, r, :, 0:ch] = left.astype(BF16)
        x3[t, r, :, ch:2 * ch] = v16
        x3[t, r, :, 2 * ch:3 * ch] = right.astype(BF16)

    cf[:, own_t, own] = pad_c[:, own_t, own].astype(F32)

    @pl.loop(1, t_dev + 1)
    def _(t):
        for r in range(1, h_dev + 1):
            build(t, r)

    def early_edges():
        for s in hr_own + hc_own:
            s[1]()
        for b in (low, high):
            cf[:, own_t, b] = pad_c[:, own_t, b].astype(F32)

        @pl.loop(1, t_dev + 1)
        def _(t):
            for r in (0, h_dev + 1):
                build(t, r)

        cw_copy.wait()

    def taps(acc, t, h0, frames):
        for a in frames:
            for b in range(3):
                acc = acc + jnp.dot(
                    x3[t + a, pl.ds(h0 + b, CH)].reshape(CH * w_dev, 3 * ch), cw[a, b],
                    preferred_element_type=F32)
        return acc

    def start_taps(t):
        @pl.loop(0, cpt)
        def _(j):
            acc = latents[t, pl.ds(j * CH, CH)].astype(F32).reshape(CH * w_dev, ch)
            acc_buf[t, j] = taps(acc, t, j * CH, [a for a in range(3) if 1 <= t + a <= t_dev])

    frame_of = {"t-": 0, "t+": t_dev + 1}

    def halo_in(side):
        f = frame_of[side]
        for r in range(h_dev):
            pad_n[f, r + 1] = norm(raw[0 if f == 0 else 1, r]).astype(BF16)
        for s in ph_h[side][0]:
            s[0]()
        ph_wt[side][1]()
        for s in ph_h[side][1]:
            s[0]()
        cf[:, f, own] = pad_c[:, f, own].astype(F32)
        for r in range(1, h_dev + 1):
            build(f, r)

    def halo_end(side):
        f = frame_of[side]
        for s in ph_h[side][0] + ph_h[side][1]:
            s[1]()
        for b in (low, high):
            cf[:, f, b] = pad_c[:, f, b].astype(F32)
        for r in (0, h_dev + 1):
            build(f, r)

    def blk_copy(t):
        return pltpu.make_async_copy(out_block.at[t], blk_hbm.at[t], loc_sem.at[4 + t_dev + t])

    def finish(t):
        for j in range(cpt):
            h0 = j * CH
            blk = taps(acc_buf[t, j], t, h0, [a for a in range(3) if not 1 <= t + a <= t_dev])
            blk = blk.astype(BF16)
            out_block[t, pl.ds(h0, CH)] = blk.reshape(CH, w_dev, ch)
            blk = blk.astype(F32)
            for k in range(ch // 128):
                fbuf[k] = blk[:, k * 128:(k + 1) * 128]
            for k in range(ch // 128):
                for dw in range(2):
                    part = fbuf[k, pl.ds(dw, CH * cols_dev, stride=2), :].astype(BF16)
                    part = part.reshape(prow, 2, cols_dev, 128)
                    for dh in range(2):
                        lo = (dh * 2 + dw) * ch + k * 128
                        pat[iw, t, pl.ds(j * prow, prow), :, lo:lo + 128] = part[:, dh]
            if t == 0:
                for i in range(CH // PH):
                    send_own(0, j * (CH // PH) + i)
        blk_copy(t).start()

    def piece(src, t, i0):
        return pat.at[src, t, pl.ds(i0, srow)]

    sides = (("w+", 0), ("w-", 1))

    def send_own(t, only=None):
        for j in range(ppt) if only is None else (only,):
            c = t * ppt + j
            p = piece(iw, t, j * srow)
            for side, i in sides:
                @pl.when(has[side])
                def _():
                    rcopy(p, p, ag_s.at[i, 0, c], ag_r.at[i, 0, c], dev[side]).start()

    def relay(t, d):
        for j in range(ppt):
            c = t * ppt + j
            for side, i in sides:
                src = iw - d if i == 0 else iw + d
                here = src >= 0 if i == 0 else src < n_w
                p = piece(src, t, j * srow)

                @pl.when(here)
                def _():
                    rcopy(p, p, ag_s.at[i, d - 1, c], ag_r.at[i, d - 1, c], dev[side]).wait_recv()
                    if d < n_w - 1:
                        @pl.when(has[side])
                        def _():
                            rcopy(p, p, ag_s.at[i, d, c], ag_r.at[i, d, c], dev[side]).start()

    pair = n_h % 2 == 0
    part_rows = pd // 2 if pair else pd
    mine = pl.ds((ih % 2) * part_rows, part_rows) if pair else pl.ds(0, pd)
    other = {"ha": ih + 1 - 2 * (ih % 2)}
    theirs = pl.ds((1 - ih % 2) * part_rows, part_rows) if pair else None

    def w_copy(d, src):
        return rcopy(w_hbm.at[:, mine], wg.at[src, :, mine], w_s.at[d], w_r.at[d],
                     {"ta": lax.rem(it + d, n_t)})

    def w_hand(d, part):
        src = lax.rem(it + n_t - d, n_t)
        return rcopy(wg.at[src, :, part], wg.at[src, :, part], wf_s.at[d], wf_r.at[d], other)

    def w_start():
        for d in range(1, n_t):
            w_copy(d, it).start()

    def w_mid():
        for d in range(1, n_t):
            w_copy(d, lax.rem(it + n_t - d, n_t)).wait_recv()
            if pair:
                w_hand(d, mine).start()

    def w_end():
        own_w.wait()
        if pair:
            for d in range(1, n_t):
                w_hand(d, theirs).wait_recv()

    def head_at(step):
        return lax.rem(it + 1 + step, n_t)

    def rim(t, a):
        lo, hi, two = pl.ds(WIN, WIN), pl.ds(rows, WIN), pl.ds(2 * a, 2)
        return [halo_kv(t, 0, a, "h-", kv.at[t, lo, two], kv.at[t, pl.ds(rows + WIN, WIN), two]),
                halo_kv(t, 1, a, "h+", kv.at[t, hi, two], kv.at[t, pl.ds(0, WIN), two])]

    def halo_kv(t, i, a, side, src, dst):
        c = rcopy(src, dst, kv_s.at[t, i, a], kv_r.at[t, i, a], dev[side])
        return has[side], has[side[0] + opp[side[1]]], c

    def qkv(t, step):
        a = head_at(step)
        x = pat[:, t].reshape(n_w * rows * cols_dev, pd)
        w = jnp.concatenate([wg[a, s] for s in range(3)], axis=1)
        y = jnp.dot(x, w, preferred_element_type=F32).astype(BF16)
        y = y.reshape(n_w, rows, cols_dev, 3 * hd)
        for s in range(n_w):
            cc = pl.ds(s * cols_dev, cols_dev)
            q_buf[t, a, :, cc, :] = y[s, :, :, 0:hd]
            kv[t, pl.ds(WIN, rows), 2 * a, cc, :] = y[s, :, :, hd:2 * hd]
            kv[t, pl.ds(WIN, rows), 2 * a + 1, cc, :] = y[s, :, :, 2 * hd:3 * hd]
        for out, _, c in rim(t, a):
            @pl.when(out)
            def _():
                c.start()

    scale = hd ** (-0.5) * 1.4426950408889634

    def window(i):
        lo = i // pc * pc // 128 * 128
        hi = min(-(-(((i + STRIP - 1) // pc + 2 * WIN + 1) * pc) // 128) * 128, 3 * WIN * pc)
        return pl.ds(lo, hi - lo)

    def attend(t, step):
        a = head_at(step)
        for _, inn, c in rim(t, a):
            @pl.when(inn)
            def _():
                c.wait_recv()
        for b in range(rows // WIN):
            r = pl.ds(b * WIN, WIN)
            kr_ = pl.ds(b * WIN, 3 * WIN)
            q = q_buf[t, a, r].reshape(WIN * pc, hd)
            k = kv[t, kr_, 2 * a].reshape(3 * WIN * pc, hd)
            v = kv[t, kr_, 2 * a + 1].reshape(3 * WIN * pc, hd)
            s_buf[b] = lax.dot_general(q, k, (((1,), (1,)), ((), ())), preferred_element_type=F32)
            inv = []
            for i in range(0, WIN * pc, STRIP):
                at = (b, pl.ds(i, STRIP), window(i))
                s = s_buf[at] + bias[at]
                m = jnp.max(s, axis=1, keepdims=True)
                e = jnp.exp2((s - m) * scale)
                inv.append(1.0 / jnp.sum(e, axis=1, keepdims=True))
                p_buf[at] = e.astype(BF16)
            o = jnp.dot(p_buf[b], v, preferred_element_type=F32)
            o = o * jnp.concatenate(inv, axis=0)
            o_buf[t, a, r] = o.astype(BF16).reshape(WIN, pc, hd)
        dst = out_att.at[it * t_dev + t]

        @pl.when(a != it)
        def _():
            rcopy(o_buf.at[t, a], dst, at_s.at[t, a], at_r.at[t, it], {"ta": a}).start()

        @pl.when(a == it)
        def _():
            pltpu.make_async_copy(o_buf.at[t, a], dst, loc_sem.at[2 + t]).start()

    ph_t["t-"][1]()
    ph_t["t+"][0]()
    w_start()

    halo_in("t-")
    if t_dev == 1:
        ph_t["t+"][1]()
        halo_in("t+")
    early_edges()
    start_taps(0)
    halo_end("t-")
    if t_dev == 1:
        halo_end("t+")
    finish(0)
    for t in range(1, t_dev):
        if t == t_dev - 1:
            ph_t["t+"][1]()
            halo_in("t+")
        start_taps(t)
        if t == t_dev - 1:
            halo_end("t+")
        finish(t)

    total_rows = rows * n_h
    bs = (WIN * pc, 3 * WIN * pc)
    qr = lax.broadcasted_iota(jnp.int32, bs, 0) // pc
    kr = lax.broadcasted_iota(jnp.int32, bs, 1) // pc - WIN
    for b in range(rows // WIN):
        kg = ih * rows + b * WIN + kr
        ok = (jnp.abs(qr - kr) <= WIN) & (kg >= 0) & (kg < total_rows)
        bias[b] = jnp.where(ok, 0.0, -1e30).astype(F32)
        p_buf[b] = jnp.zeros(bs, BF16)

    for d in range(1, n_w - 1):
        relay(0, d)
    if t_dev > 1:
        send_own(1)
    w_mid()
    if n_w > 1:
        relay(0, n_w - 1)
    w_end()
    for t in range(t_dev):
        more = t + 1 < t_dev
        if more:
            @pl.loop(0, n_t)
            def _(step):
                qkv(t, step)
            steps = max(n_w - 2, 1)
            for d in range(1, steps + 1):
                if d < n_w - 1:
                    relay(t + 1, d)

                @pl.loop(n_t * (d - 1) // steps, n_t * d // steps)
                def _(step):
                    attend(t, step)
        else:
            qkv(t, 0)

            @pl.loop(0, n_t - 1)
            def _(step):
                qkv(t, step + 1)
                attend(t, step)
            attend(t, n_t - 1)
        if more:
            if t + 2 < t_dev:
                send_own(t + 2)
            if n_w > 1:
                relay(t + 1, n_w - 1)

    for t in range(t_dev):
        blk_copy(t).wait()
        pltpu.make_async_copy(o_buf.at[t, it], out_att.at[it * t_dev + t], loc_sem.at[2 + t]).wait()
        for d in range(1, n_t):
            src = lax.rem(it + d, n_t)
            rcopy(o_buf.at[t, src], out_att.at[src * t_dev + t], at_s.at[t, src], at_r.at[t, src],
                  {"ta": src}).wait()
        for a in range(n_t):
            for out, _, c in rim(t, a):
                @pl.when(out)
                def _():
                    c.wait_send()
    for s in (ph_w + list(ph_t.values()) + list(ph_wt.values()) + hr_own + hc_own
              + ph_h["t-"][0] + ph_h["t-"][1] + ph_h["t+"][0] + ph_h["t+"][1]):
        s[2]()
    for d in range(1, n_t):
        w_copy(d, it).wait_send()
        if pair:
            w_hand(d, mine).wait_send()
    for t in range(t_dev):
        for j in range(ppt):
            c = t * ppt + j
            for side, i in sides:
                for d in range(n_w - 1):
                    src = iw - d if i == 0 else iw + d
                    here = src >= 0 if i == 0 else src < n_w
                    p = piece(src, t, j * srow)

                    @pl.when(here & has[side])
                    def _():
                        rcopy(p, p, ag_s.at[i, d, c], ag_r.at[i, d, c], dev[side]).wait_send()


def results(block, att, out_block, out_att, sem):
    copies = [pltpu.make_async_copy(block, out_block, sem.at[0]),
              pltpu.make_async_copy(att, out_att, sem.at[1])]
    for c in copies:
        c.start()
    for c in copies:
        c.wait()


def local(latents, norm_gain, conv_weight, qkv_weight):
    n_t, n_h, n_w = (lax.axis_size(a) for a in ("ta", "ha", "wa"))
    t_dev, h_dev, w_dev, ch = latents.shape
    rows, cols_dev = h_dev // 2, w_dev // 2
    pd, head_dev, qkv_count, hd = qkv_weight.shape
    pc = n_w * cols_dev
    cw = conv_weight.reshape(3, 3, 3 * ch, ch)
    w2 = qkv_weight.transpose(1, 2, 0, 3).reshape(qkv_count, pd, hd)
    frames = n_t * t_dev
    chunks = t_dev * (h_dev // PH)
    vm = pl.BlockSpec(memory_space=pltpu.VMEM)
    hbm = pl.BlockSpec(memory_space=pltpu.HBM)
    dma = pltpu.SemaphoreType.DMA
    block_out, att = pl.pallas_call(
        functools.partial(kernel, n_t, n_h, n_w),
        out_shape=(jax.ShapeDtypeStruct(latents.shape, BF16),
                   jax.ShapeDtypeStruct((frames, rows, pc, hd), BF16)),
        in_specs=[hbm, hbm, hbm, hbm],
        out_specs=(hbm, hbm),
        scratch_shapes=[
            pltpu.VMEM(latents.shape, BF16),
            pltpu.VMEM(latents.shape, BF16),
            pltpu.VMEM((1, ch), F32),
            pltpu.VMEM((2, h_dev, w_dev, ch), BF16),
            pltpu.VMEM((t_dev + 2, h_dev + 2, w_dev, ch), BF16),
            pltpu.VMEM((2, t_dev, h_dev, ch), F32),
            pltpu.VMEM((2, t_dev, h_dev, ch), BF16),
            pltpu.VMEM((2, t_dev + 2, 3 * h_dev, ch), BF16),
            pltpu.VMEM((2, t_dev + 2, 3 * h_dev, ch), F32),
            pltpu.VMEM((t_dev + 2, h_dev + 2, w_dev, 3 * ch), BF16),
            pltpu.VMEM((t_dev, h_dev // CH, CH * w_dev, ch), F32),
            pltpu.VMEM((3, 3, 3 * ch, ch), BF16),
            pltpu.VMEM((n_t, qkv_count, pd, hd), BF16),
            pltpu.VMEM((ch // 128, CH * w_dev, 128), F32),
            pltpu.VMEM((n_w, t_dev, rows, cols_dev, pd), BF16),
            pltpu.VMEM((t_dev, n_t, rows, pc, hd), BF16),
            pltpu.VMEM((t_dev, rows + 2 * WIN, 2 * n_t, pc, hd), BF16),
            pltpu.VMEM((rows // WIN, WIN * pc, 3 * WIN * pc), F32),
            pltpu.VMEM((rows // WIN, WIN * pc, 3 * WIN * pc), F32),
            pltpu.VMEM((rows // WIN, WIN * pc, 3 * WIN * pc), BF16),
            pltpu.VMEM((t_dev, n_t, rows, pc, hd), BF16),
            dma((4 + 2 * t_dev,)),
            dma((18,)), dma((18,)),
            dma((n_t,)), dma((n_t,)),
            dma((n_t,)), dma((n_t,)),
            dma((2, n_w, chunks)), dma((2, n_w, chunks)),
            dma((t_dev, 2, n_t)), dma((t_dev, 2, n_t)),
            dma((t_dev, n_t)), dma((t_dev, n_t)),
        ],
        compiler_params=pltpu.CompilerParams(
            collective_id=0, has_side_effects=True, vmem_limit_bytes=58 * 1024 * 1024),
    )(latents, norm_gain.reshape(1, ch), cw, w2)
    block_out, att = pl.pallas_call(
        results,
        out_shape=(jax.ShapeDtypeStruct(block_out.shape, BF16), jax.ShapeDtypeStruct(att.shape, BF16)),
        in_specs=[vm, vm],
        out_specs=(hbm, hbm),
        scratch_shapes=[dma((2,))],
    )(block_out, att)
    return block_out, att.reshape(frames, rows, pc, head_dev, hd)


def solution(mesh):
    return jax.shard_map(
        local,
        mesh=mesh,
        in_specs=(P("ta", "ha", "wa", None), P(), P(), P(None, ("ta", "wa"), None, None)),
        out_specs=(P("ta", "ha", "wa", None), P(None, "ha", None, ("ta", "wa"), None)),
        check_vma=False,
    )
```
